32 devices in a mesh: dp: 16 (over z, x, core), pipe: 2 (over y).
Axes of the slice: x: 2, y: 2, z: 4, core: 2. Of those that a mesh axis runs over, the one named last changes fastest.
Arguments:
- acts: bfloat16 [2, 2, 1024, 4224], P('pipe', None, 'dp'), may hold values from -6 to 6
- out_grad: bfloat16 [2, 1024, 4224], P(None, 'dp'), may hold values from -6 to 6
- params: bfloat16 [2, 768, 4224], P('pipe'), may hold values from -0.09375 to 0.09375
- moment: float32 [2, 1081344], P('pipe', 'dp'), may hold values from -2 to 2
- second: float32 [2, 1081344], P('pipe', 'dp'), may hold values from 0.0001 to 0.01
Outputs:
- in_grad: bfloat16 [2, 2, 1024, 4224], P('pipe', None, 'dp')
- new_moment: float32 [2, 1081344], P('pipe', 'dp')
- new_second: float32 [2, 1081344], P('pipe', 'dp')
- update: float32 [2, 1081344], P('pipe', 'dp')
The draws below stay inside these ranges and needn't reach their ends.
All inputs are finite; a program needn't handle non-finite values.
Results may differ from the reference program's by a relative error of at most 0.0056.
Values may be sent and summed in bfloat16 or wider, within the bound.
A program may use at most 64 MiB of HBM per device.

```python
import math
import jax
import jax.numpy as jnp

D = 4224
BLOCK = 256
MICRO = 2
TOKENS = 1024
SECTIONS = 2


def block_levels(own_key, shape, cuts, low, largest):
    gain = 1.0
    for axis_at, blocks in cuts:
        draws = jax.random.uniform(jax.random.fold_in(jax.random.fold_in(own_key, 6), axis_at), (blocks,), jnp.float32, low / len(cuts), largest / len(cuts))
        gain = gain * jnp.repeat(jnp.exp(draws), shape[axis_at] // blocks).reshape((-1,) + (1,) * (len(shape) - 1 - axis_at))
    return gain


def noise(stream_key, dims, spread, limit, shards=(), dtype=jnp.bfloat16):
    array = jax.random.normal(stream_key, dims, jnp.float32) * spread
    if len(shards) > 0:
        array = block_levels(stream_key, dims, shards, -0.22, 0.18) * array
    return jnp.clip(array, min=-limit, max=limit).astype(dtype)


def setup_inputs(seed: int = 0) -> dict:
    splits = jax.random.split(jax.random.key(seed), 6)
    acts = noise(splits[0], (SECTIONS, MICRO, TOKENS, D), 1.0, 6.0, ((0, 2), (2, 16)))
    out_grad = noise(splits[1], (MICRO, TOKENS, D), 1.0, 6.0, ((1, 16),))
    params = noise(splits[2], (SECTIONS, 3 * BLOCK, D), D ** -0.5, 0.09375, ((0, 2),))
    moment = noise(splits[3], (SECTIONS, BLOCK * D), 0.3, 2.0, ((0, 2), (1, 16)), jnp.float32)
    second = jnp.clip(jnp.exp(math.log(0.01) - 4.6051702 * jax.random.uniform(splits[4], (SECTIONS, BLOCK * D), jnp.float32) ** block_levels(splits[4], (SECTIONS, BLOCK * D), ((0, 2), (1, 16)), -0.2, 0.2)), 0.0001, 0.01)
    return {"acts": acts, "out_grad": out_grad, "params": params, "moment": moment, "second": second}


def section_back(inputs, grad_rows, weights):
    block_size = weights.shape[0] // 3
    weights_in = weights[:2 * block_size]
    weights_down = weights[2 * block_size:]
    gate_up = jnp.dot(inputs, weights_in.T, preferred_element_type=jnp.float32)
    gate_values = gate_up[:, :block_size]
    up_values = gate_up[:, block_size:]
    sigmoid_gate = jax.nn.sigmoid(gate_values)
    activated = gate_values * sigmoid_gate
    d_hidden = jnp.dot(grad_rows, weights_down.T, preferred_element_type=jnp.float32)
    d_gate = d_hidden * up_values * sigmoid_gate * (1.0 + gate_values * (1.0 - sigmoid_gate))
    d_up = d_hidden * activated
    d_gate_up = jnp.concatenate([d_gate, d_up], axis=1).astype(jnp.bfloat16)
    hidden = (activated * up_values).astype(jnp.bfloat16)
    passed = grad_rows.astype(jnp.float32) + jnp.dot(d_gate_up, weights_in, preferred_element_type=jnp.float32)
    return (passed.astype(jnp.bfloat16), hidden)

def reference(acts, out_grad, params, moment, second):
    section_count = acts.shape[0]
    micro_count = acts.shape[1]
    grad_scale = float(micro_count * acts.shape[2]) ** (-0.5)
    block_size = params.shape[1] // 3
    totals = [jnp.zeros((block_size, params.shape[2]), jnp.float32) for _ in range(section_count)]
    passed_all = [[None] * micro_count for _ in range(section_count)]
    for micro_index in range(micro_count):
        grad_rows = out_grad[micro_index]
        for section_index in reversed(range(section_count)):
            inputs = acts[section_index, micro_index]
            passed, hidden = section_back(inputs, grad_rows, params[section_index])
            term = jnp.dot(hidden.T, grad_rows, preferred_element_type=jnp.float32)
            totals[section_index] = totals[section_index] + term
            passed_all[section_index][micro_index] = passed
            grad_rows = passed
    in_grad = jnp.stack([jnp.stack(passed_all[section_index]) for section_index in range(section_count)])
    gradient = jnp.stack(totals).reshape(section_count, -1) * grad_scale
    new_moment = 0.9 * moment + 0.1 * gradient
    new_second = 0.999 * second + 0.001 * gradient * gradient
    update = new_moment / (1.0 - 0.9 ** 10) / (jnp.sqrt(new_second / (1.0 - 0.999 ** 10)) + 1e-08)
    return (in_grad, new_moment, new_second, update)
```

```python
import functools

import jax
import jax.numpy as jnp
from jax import lax
from jax.experimental import pallas as pl
from jax.experimental.pallas import tpu as pltpu
from jax.sharding import PartitionSpec as P

MESH = pl.DeviceIdType.MESH
NT = (((1,), (1,)), ((), ()))


def chunk_width(width):
    return max((w for w in (128, 256, 384, 512) if width % w == 0), default=0)


def kernel(dims, x_hbm, g_hbm, w_hbm, m_ref, s_ref, out_hbm, nm_ref, ns_ref, up_ref,
           x, g, w, ig, gu, dh, hid, dgu, part, r1, send2, own, r2, send3, r3,
           load_x, load_g, load_w, store, sy, ry, s1, q1, s2, q2, s3, q3):
    sections, count, cols, chunks, rows, grad_scale = dims
    depth = count // 4
    block = hid.shape[0]
    sec = lax.axis_index("pipe")
    me = lax.axis_index("dp")
    core, xx, zz = lax.rem(me, 2), lax.rem(me // 2, 2), me // 4
    last = sec == sections - 1
    core_peer = me + 1 - 2 * core
    x_peer = me + 2 - 4 * xx
    z_peers = [me + 4 * (lax.rem(zz + j, depth) - zz) for j in range(1, depth)]

    def at(c):
        return pl.ds(pl.multiple_of(c * cols, cols), cols)

    def loads(c):
        return (pltpu.make_async_copy(w_hbm.at[:, at(c)], w.at[:, at(c)], load_w.at[c]),
                pltpu.make_async_copy(x_hbm.at[:, at(c)], x.at[:, at(c)], load_x.at[c]))

    def load_grad(c):
        return pltpu.make_async_copy(g_hbm.at[:, at(c)], g.at[:, at(c)], load_g.at[c])

    def relay(c):
        return pltpu.make_async_remote_copy(
            ig.at[:, at(c)], g.at[:, at(c)], sy.at[c], ry.at[c],
            device_id={"pipe": lax.max(sec - 1, 0), "dp": me}, device_id_type=MESH)

    def stage1(c):
        return pltpu.make_async_remote_copy(
            part.at[1 - core, :, :, :, at(c)], r1.at[:, :, :, at(c)], s1.at[c], q1.at[c],
            device_id={"pipe": sec, "dp": core_peer}, device_id_type=MESH)

    def stage2(c):
        return pltpu.make_async_remote_copy(
            send2.at[:, :, at(c)], r2.at[:, :, at(c)], s2.at[c], q2.at[c],
            device_id={"pipe": sec, "dp": x_peer}, device_id_type=MESH)

    def stage3(c, j):
        return pltpu.make_async_remote_copy(
            send3.at[lax.rem(zz + j + 1, depth), :, at(c)], r3.at[j, :, at(c)], s3.at[j, c], q3.at[j, c],
            device_id={"pipe": sec, "dp": z_peers[j]}, device_id_type=MESH)

    def result(c):
        return pltpu.make_async_copy(ig.at[:, at(c)], out_hbm.at[:, at(c)], store.at[c])

    def each(body, low=0, high=chunks):
        def step(c, carry):
            body(c)
            return carry
        lax.fori_loop(low, high, step, 0)

    barrier = pltpu.get_barrier_semaphore()
    for peer in [core_peer, x_peer] + z_peers:
        pl.semaphore_signal(barrier, inc=1, device_id={"pipe": sec, "dp": peer}, device_id_type=MESH)

    @pl.when(sec > 0)
    def _():
        pl.semaphore_signal(barrier, inc=1, device_id={"pipe": lax.max(sec - 1, 0), "dp": me}, device_id_type=MESH)

    @pl.when(jnp.logical_not(last))
    def _():
        pl.semaphore_signal(barrier, inc=1, device_id={"pipe": lax.min(sec + 1, sections - 1), "dp": me}, device_id_type=MESH)

    def begin(c):
        for copy in loads(c):
            copy.start()

        @pl.when(last)
        def _():
            load_grad(c).start()

    each(begin)
    gu[...] = jnp.zeros_like(gu)
    dh[...] = jnp.zeros_like(dh)

    def add_hidden_grad(c):
        dh[...] += lax.dot_general(g[:, at(c)], w[2 * block:, at(c)], NT, preferred_element_type=jnp.float32)

    def forward(c):
        for copy in loads(c):
            copy.wait()
        gu[...] += lax.dot_general(x[:, at(c)], w[: 2 * block, at(c)], NT, preferred_element_type=jnp.float32)

        @pl.when(last)
        def _():
            load_grad(c).wait()
            add_hidden_grad(c)

    each(forward)
    gate, up = gu[:, :block], gu[:, block:]
    hid[...] = (gate * jax.nn.sigmoid(gate) * up).T.astype(jnp.bfloat16)

    pl.semaphore_wait(barrier, 1 + depth + lax.min(sec, 1) + lax.min(sections - 1 - sec, 1))

    def input_grad():
        gate_v, up_v, d = gu[:, :block], gu[:, block:], dh[...]
        sg = jax.nn.sigmoid(gate_v)
        dgu[:, :block] = (d * up_v * sg * (1.0 + gate_v * (1.0 - sg))).astype(jnp.bfloat16)
        dgu[:, block:] = (d * gate_v * sg).astype(jnp.bfloat16)

        def one(c):
            ig[:, at(c)] = (g[:, at(c)].astype(jnp.float32) + jnp.dot(
                dgu[...], w[: 2 * block, at(c)], preferred_element_type=jnp.float32)).astype(jnp.bfloat16)

            @pl.when(sec > 0)
            def _():
                relay(c).start()

            result(c).start()

        each(one)

    @pl.when(last)
    def _():
        input_grad()

    def step(t):
        @pl.when(t < chunks)
        def _():
            @pl.when(jnp.logical_not(last))
            def _():
                relay(t).wait_recv()

            term = jnp.dot(hid[...], g[:, at(t)], preferred_element_type=jnp.float32)
            for owner in range(count):
                part[owner % 2, owner // 2 % 2, owner // 4, :, at(t)] = term[
                    owner * rows:(owner + 1) * rows].astype(jnp.bfloat16)
            stage1(t).start()

            @pl.when(jnp.logical_not(last))
            def _():
                add_hidden_grad(t)

        @pl.when(jnp.logical_and(t >= 1, t <= chunks))
        def _():
            c = t - 1
            stage1(c).wait_recv()
            for z in range(depth):
                send2[z, :, at(c)] = (part[core, 1 - xx, z, :, at(c)].astype(jnp.float32)
                                      + r1[1 - xx, z, :, at(c)].astype(jnp.float32)).astype(jnp.bfloat16)
            stage2(c).start()
            for z in range(depth):
                own[z, :, at(c)] = (part[core, xx, z, :, at(c)].astype(jnp.float32)
                                    + r1[xx, z, :, at(c)].astype(jnp.float32))

        @pl.when(jnp.logical_and(t >= 2, t <= chunks + 1))
        def _():
            c = t - 2
            stage2(c).wait_recv()
            for z in range(depth):
                total = own[z, :, at(c)] + r2[z, :, at(c)].astype(jnp.float32)
                own[z, :, at(c)] = total
                send3[z, :, at(c)] = total.astype(jnp.bfloat16)
            for j in range(depth - 1):
                stage3(c, j).start()

        @pl.when(jnp.logical_and(t == chunks, jnp.logical_not(last)))
        def _():
            input_grad()

        @pl.when(t >= 3)
        def _():
            c = t - 3
            total = own[zz, :, at(c)]
            for j in range(depth - 1):
                stage3(c, j).wait_recv()
            for j in range(depth - 1):
                total = total + r3[j, :, at(c)].astype(jnp.float32)
            grad = total * grad_scale
            lanes = cols // 128
            for k in range(lanes):
                part_g = grad[:, k * 128:(k + 1) * 128]
                where = pl.ds(c * lanes + k, rows, stride=chunks * lanes)
                new_m = 0.9 * m_ref[where, :] + 0.1 * part_g
                new_s = 0.999 * s_ref[where, :] + 0.001 * part_g * part_g
                nm_ref[where, :] = new_m
                ns_ref[where, :] = new_s
                up_ref[where, :] = new_m / (1.0 - 0.9**10) / (jnp.sqrt(new_s / (1.0 - 0.999**10)) + 1e-08)

    each(step, 0, chunks + 3)

    def finish(c):
        stage1(c).wait_send()
        stage2(c).wait_send()
        for j in range(depth - 1):
            stage3(c, j).wait_send()

        @pl.when(sec > 0)
        def _():
            relay(c).wait_send()

        result(c).wait()

    each(finish)


def fused(acts, out_grad, params, moment, second):
    sections, count = lax.axis_size("pipe"), lax.axis_size("dp")
    _, micro, tok, width = acts.shape
    tall = params.shape[1]
    block = tall // 3
    total_rows = micro * tok
    cols = chunk_width(width)
    chunks = width // cols
    rows = block // count
    depth = count // 4
    flat = (rows * width // 128, 128)
    grad_scale = float(total_rows * count) ** (-0.5)
    bf, f32 = jnp.bfloat16, jnp.float32
    dma = pltpu.SemaphoreType.DMA
    anywhere = pl.BlockSpec(memory_space=pl.ANY)
    vmem = pl.BlockSpec(memory_space=pltpu.VMEM)
    in_grad, nm, ns, up = pl.pallas_call(
        functools.partial(kernel, (sections, count, cols, chunks, rows, grad_scale)),
        out_shape=[jax.ShapeDtypeStruct((total_rows, width), bf)] + [jax.ShapeDtypeStruct(flat, f32)] * 3,
        in_specs=[anywhere] * 3 + [vmem] * 2,
        out_specs=[anywhere] + [vmem] * 3,
        scratch_shapes=[
            pltpu.VMEM((total_rows, width), bf),
            pltpu.VMEM((total_rows, width), bf),
            pltpu.VMEM((tall, width), bf),
            pltpu.VMEM((total_rows, width), bf),
            pltpu.VMEM((total_rows, 2 * block), f32),
            pltpu.VMEM((total_rows, block), f32),
            pltpu.VMEM((block, total_rows), bf),
            pltpu.VMEM((total_rows, 2 * block), bf),
            pltpu.VMEM((2, 2, depth, rows, width), bf),
            pltpu.VMEM((2, depth, rows, width), bf),
            pltpu.VMEM((depth, rows, width), bf),
            pltpu.VMEM((depth, rows, width), f32),
            pltpu.VMEM((depth, rows, width), bf),
            pltpu.VMEM((depth, rows, width), bf),
            pltpu.VMEM((depth - 1, rows, width), bf),
            dma((chunks,)), dma((chunks,)), dma((chunks,)), dma((chunks,)),
            dma((chunks,)), dma((chunks,)),
            dma((chunks,)), dma((chunks,)),
            dma((chunks,)), dma((chunks,)),
            dma((depth - 1, chunks)), dma((depth - 1, chunks)),
        ],
        compiler_params=pltpu.CompilerParams(
            collective_id=0, has_side_effects=True, vmem_limit_bytes=48 * 1024 * 1024),
        cost_estimate=pl.CostEstimate(
            flops=12 * total_rows * block * width, bytes_accessed=2 * tall * width + 10 * total_rows * width,
            transcendentals=total_rows * block),
    )(acts.reshape(total_rows, width), out_grad.reshape(total_rows, width), params[0],
      moment.reshape(flat), second.reshape(flat))
    return (in_grad.reshape(acts.shape), nm.reshape(moment.shape), ns.reshape(moment.shape), up.reshape(moment.shape))


def fits(sizes, acts, params):
    count, block = sizes["dp"], params.shape[1] // 3
    micro_rows = acts.shape[1] * acts.shape[2] // count
    return (count % 4 == 0 and count >= 8 and block % (16 * count) == 0 and block % 128 == 0
            and micro_rows % 128 == 0 and acts.shape[2] // count % 16 == 0 and chunk_width(acts.shape[3]) > 0)


def from_behind(value, axis, steps):
    count = lax.axis_size(axis)
    leading, last = (max(0, -steps), min(count, count - steps))
    return lax.ppermute(value, axis, [(source, source + steps) for source in range(leading, last)])


def backward(inputs, grad_rows, weights_in, weights_down):
    block_size = weights_down.shape[0]
    gate_up = lax.dot_general(
        inputs, weights_in, (((1,), (1,)), ((), ())), preferred_element_type=jnp.float32
    )
    gate_values = gate_up[:, :block_size]
    up_values = gate_up[:, block_size:]
    sigmoid_gate = jax.nn.sigmoid(gate_values)
    activated = gate_values * sigmoid_gate
    d_hidden = lax.dot_general(
        grad_rows, weights_down, (((1,), (1,)), ((), ())), preferred_element_type=jnp.float32
    )
    d_gate = d_hidden * up_values * sigmoid_gate * (1.0 + gate_values * (1.0 - sigmoid_gate))
    d_up = d_hidden * activated
    d_gate_up = jnp.concatenate([d_gate, d_up], axis=1).astype(jnp.bfloat16)
    hidden = (activated * up_values).astype(jnp.bfloat16)
    passed = grad_rows.astype(jnp.float32) + jnp.dot(
        d_gate_up, weights_in, preferred_element_type=jnp.float32
    )
    return (passed.astype(jnp.bfloat16), hidden)


def place_slot(stack, value, slot_index, active):
    previous = lax.dynamic_index_in_dim(stack, slot_index, 0, keepdims=False)
    return lax.dynamic_update_index_in_dim(stack, jnp.where(active, value, previous), slot_index, 0)


def weight_terms(hidden, grad_rows):
    lower = lax.dot_general(
        hidden, grad_rows, (((0,), (0,)), ((), ())), preferred_element_type=jnp.float32
    )
    return lower.reshape(-1)


def local(acts, out_grad, params, moment, second):
    sections = lax.axis_size("pipe")
    section_index = lax.axis_index("pipe")
    inputs = acts[0]
    micro_count = inputs.shape[0]
    tok_rows = inputs.shape[1]
    weights = params[0]
    block_size = weights.shape[0] // 3
    weights_in = weights[: 2 * block_size]
    weights_down = weights[2 * block_size :]
    in_grads = jnp.zeros_like(inputs)
    arrived = jnp.zeros_like(inputs)
    hiddens = jnp.zeros((micro_count, tok_rows, block_size), jnp.bfloat16)
    incoming = jnp.zeros_like(inputs[0])
    tick_count = sections + micro_count - 1
    for tick_index in range(tick_count):
        offset = tick_index - (sections - 1) + section_index
        active = jnp.logical_and(offset >= 0, offset < micro_count)
        slot_index = jnp.clip(offset, 0, micro_count - 1)
        current = lax.dynamic_index_in_dim(inputs, slot_index, 0, keepdims=False)
        top_grad = lax.dynamic_index_in_dim(out_grad, slot_index, 0, keepdims=False)
        grad_rows = jnp.where(section_index == sections - 1, top_grad, incoming)

        def working(current=current, grad_rows=grad_rows):
            return backward(current, grad_rows, weights_in, weights_down)

        def resting(current=current):
            return (jnp.zeros_like(current), jnp.zeros((tok_rows, block_size), jnp.bfloat16))

        passed, hidden = lax.cond(active, working, resting)
        in_grads = place_slot(in_grads, passed, slot_index, active)
        arrived = place_slot(arrived, grad_rows, slot_index, active)
        hiddens = place_slot(hiddens, hidden, slot_index, active)
        if tick_index + 1 < tick_count:
            incoming = from_behind(passed, "pipe", -1)
    row_count = micro_count * tok_rows
    term = weight_terms(hiddens.reshape(row_count, block_size), arrived.reshape(row_count, -1))
    summed = lax.psum_scatter(term, "dp", scatter_dimension=0, tiled=True)
    grad_scale = float(row_count * lax.axis_size("dp")) ** (-0.5)
    gradient = summed * grad_scale
    new_moment = 0.9 * moment[0] + 0.1 * gradient
    new_second = 0.999 * second[0] + 0.001 * gradient * gradient
    update = new_moment / (1.0 - 0.9**10) / (jnp.sqrt(new_second / (1.0 - 0.999**10)) + 1e-08)
    return (in_grads[None], new_moment[None], new_second[None], update[None])


def solution(mesh):
    placed = (
        P("pipe", None, "dp", None),
        P(None, "dp", None),
        P("pipe", None, None),
        P("pipe", "dp"),
        P("pipe", "dp"),
    )
    outs = (P("pipe", None, "dp", None), P("pipe", "dp"), P("pipe", "dp"), P("pipe", "dp"))

    def run(acts, out_grad, params, moment, second):
        body = fused if fits(mesh.shape, acts, params) else local
        return jax.shard_map(body, mesh=mesh, in_specs=placed, out_specs=outs, check_vma=False)(
            acts, out_grad, params, moment, second)

    return run
```

```python
import functools

import jax
import jax.numpy as jnp
from jax import lax
from jax.experimental import pallas as pl
from jax.experimental.pallas import tpu as pltpu
from jax.sharding import PartitionSpec as P

MESH = pl.DeviceIdType.MESH
NT = (((1,), (1,)), ((), ()))


def chunk_width(width):
    return max((w for w in (128, 256, 384, 512) if width % w == 0), default=0)


def kernel(dims, x_hbm, g_hbm, w_hbm, out_hbm, grad_ref,
           x, g, w, ig, gu, dh, hid, dgu, part, r1, send2, own, r2, send3, r3,
           load_x, load_g, load_w, store, sy, ry, s1, q1, s2, q2, s3, q3):
    sections, count, cols, chunks, rows, grad_scale = dims
    depth = count // 4
    block = hid.shape[0]
    sec = lax.axis_index("pipe")
    me = lax.axis_index("dp")
    core, xx, zz = lax.rem(me, 2), lax.rem(me // 2, 2), me // 4
    last = sec == sections - 1
    core_peer = me + 1 - 2 * core
    x_peer = me + 2 - 4 * xx
    z_peers = [me + 4 * (lax.rem(zz + j, depth) - zz) for j in range(1, depth)]

    def at(c):
        return pl.ds(pl.multiple_of(c * cols, cols), cols)

    def loads(c):
        return (pltpu.make_async_copy(w_hbm.at[:, at(c)], w.at[c], load_w.at[c]),
                pltpu.make_async_copy(x_hbm.at[:, at(c)], x.at[c], load_x.at[c]))

    def load_grad(c):
        return pltpu.make_async_copy(g_hbm.at[:, at(c)], g.at[c], load_g.at[c])

    def relay(c):
        return pltpu.make_async_remote_copy(
            ig.at[c], g.at[c], sy.at[c], ry.at[c],
            device_id={"pipe": lax.max(sec - 1, 0), "dp": me}, device_id_type=MESH)

    def stage1(c):
        return pltpu.make_async_remote_copy(
            part.at[c, 1 - core], r1.at[c], s1.at[c], q1.at[c],
            device_id={"pipe": sec, "dp": core_peer}, device_id_type=MESH)

    def stage2(c):
        return pltpu.make_async_remote_copy(
            send2.at[c], r2.at[c], s2.at[c], q2.at[c],
            device_id={"pipe": sec, "dp": x_peer}, device_id_type=MESH)

    def stage3(c, j):
        return pltpu.make_async_remote_copy(
            send3.at[c, lax.rem(zz + j + 1, depth)], r3.at[c, j], s3.at[j, c], q3.at[j, c],
            device_id={"pipe": sec, "dp": z_peers[j]}, device_id_type=MESH)

    def result(c):
        return pltpu.make_async_copy(ig.at[c], out_hbm.at[:, at(c)], store.at[c])

    def each(body, low=0, high=chunks):
        def step(c, carry):
            body(c)
            return carry
        lax.fori_loop(low, high, step, 0)

    barrier = pltpu.get_barrier_semaphore()
    for peer in [core_peer, x_peer] + z_peers:
        pl.semaphore_signal(barrier, inc=1, device_id={"pipe": sec, "dp": peer}, device_id_type=MESH)

    @pl.when(sec > 0)
    def _():
        pl.semaphore_signal(barrier, inc=1, device_id={"pipe": lax.max(sec - 1, 0), "dp": me}, device_id_type=MESH)

    @pl.when(jnp.logical_not(last))
    def _():
        pl.semaphore_signal(barrier, inc=1, device_id={"pipe": lax.min(sec + 1, sections - 1), "dp": me}, device_id_type=MESH)

    def begin(c):
        for copy in loads(c):
            copy.start()

        @pl.when(last)
        def _():
            load_grad(c).start()

    each(begin)
    gu[...] = jnp.zeros_like(gu)
    dh[...] = jnp.zeros_like(dh)

    def add_hidden_grad(c):
        dh[...] += lax.dot_general(g[c], w[c, 2 * block:, :], NT, preferred_element_type=jnp.float32)

    def forward(c):
        for copy in loads(c):
            copy.wait()
        gu[...] += lax.dot_general(x[c], w[c, : 2 * block, :], NT, preferred_element_type=jnp.float32)

        @pl.when(last)
        def _():
            load_grad(c).wait()
            add_hidden_grad(c)

    each(forward)
    gate, up = gu[:, :block], gu[:, block:]
    hid[...] = (gate * jax.nn.sigmoid(gate) * up).T.astype(jnp.bfloat16)

    pl.semaphore_wait(barrier, 1 + depth + lax.min(sec, 1) + lax.min(sections - 1 - sec, 1))

    def input_grad():
        gate_v, up_v, d = gu[:, :block], gu[:, block:], dh[...]
        sg = jax.nn.sigmoid(gate_v)
        dgu[:, :block] = (d * up_v * sg * (1.0 + gate_v * (1.0 - sg))).astype(jnp.bfloat16)
        dgu[:, block:] = (d * gate_v * sg).astype(jnp.bfloat16)

        def one(c):
            ig[c] = (g[c].astype(jnp.float32) + jnp.dot(
                dgu[...], w[c, : 2 * block, :], preferred_element_type=jnp.float32)).astype(jnp.bfloat16)

            @pl.when(sec > 0)
            def _():
                relay(c).start()

            result(c).start()

        each(one)

    @pl.when(last)
    def _():
        input_grad()

    def step(t):
        @pl.when(t < chunks)
        def _():
            @pl.when(jnp.logical_not(last))
            def _():
                relay(t).wait_recv()

            term = jnp.dot(hid[...], g[t], preferred_element_type=jnp.float32)
            for owner in range(count):
                part[t, owner % 2, owner // 2 % 2, owner // 4] = term[
                    owner * rows:(owner + 1) * rows].astype(jnp.bfloat16)
            stage1(t).start()

            @pl.when(jnp.logical_not(last))
            def _():
                add_hidden_grad(t)

        @pl.when(jnp.logical_and(t >= 1, t <= chunks))
        def _():
            c = t - 1
            stage1(c).wait_recv()
            for z in range(depth):
                send2[c, z] = (part[c, core, 1 - xx, z].astype(jnp.float32)
                                      + r1[c, 1 - xx, z].astype(jnp.float32)).astype(jnp.bfloat16)
            stage2(c).start()
            for z in range(depth):
                own[c, z] = (part[c, core, xx, z].astype(jnp.float32)
                                    + r1[c, xx, z].astype(jnp.float32))

        @pl.when(jnp.logical_and(t >= 2, t <= chunks + 1))
        def _():
            c = t - 2
            stage2(c).wait_recv()
            for z in range(depth):
                total = own[c, z] + r2[c, z].astype(jnp.float32)
                own[c, z] = total
                send3[c, z] = total.astype(jnp.bfloat16)
            for j in range(depth - 1):
                stage3(c, j).start()

        @pl.when(jnp.logical_and(t == chunks, jnp.logical_not(last)))
        def _():
            input_grad()

        @pl.when(t >= 3)
        def _():
            c = t - 3
            total = own[c, zz]
            for j in range(depth - 1):
                stage3(c, j).wait_recv()
            for j in range(depth - 1):
                total = total + r3[c, j].astype(jnp.float32)
            grad = total * grad_scale
            lanes = cols // 128
            for k in range(lanes):
                where = pl.ds(c * lanes + k, rows, stride=chunks * lanes)
                grad_ref[where, :] = grad[:, k * 128:(k + 1) * 128]

    each(step, 0, chunks + 3)

    def finish(c):
        stage1(c).wait_send()
        stage2(c).wait_send()
        for j in range(depth - 1):
            stage3(c, j).wait_send()

        @pl.when(sec > 0)
        def _():
            relay(c).wait_send()

        result(c).wait()

    each(finish)


def finish_kernel(sent_hbm, grad_ref, m_ref, s_ref, out_hbm, nm_ref, ns_ref, up_ref, sem):
    copy = pltpu.make_async_copy(sent_hbm, out_hbm, sem)
    copy.start()
    grad = grad_ref[...]
    new_m = 0.9 * m_ref[...] + 0.1 * grad
    new_s = 0.999 * s_ref[...] + 0.001 * grad * grad
    nm_ref[...] = new_m
    ns_ref[...] = new_s
    up_ref[...] = new_m / (1.0 - 0.9**10) / (jnp.sqrt(new_s / (1.0 - 0.999**10)) + 1e-08)
    copy.wait()


def fused(acts, out_grad, params, moment, second):
    sections, count = lax.axis_size("pipe"), lax.axis_size("dp")
    _, micro, tok, width = acts.shape
    tall = params.shape[1]
    block = tall // 3
    total_rows = micro * tok
    cols = chunk_width(width)
    chunks = width // cols
    rows = block // count
    depth = count // 4
    flat = (rows * width // 128, 128)
    grad_scale = float(total_rows * count) ** (-0.5)
    bf, f32 = jnp.bfloat16, jnp.float32
    dma = pltpu.SemaphoreType.DMA
    anywhere = pl.BlockSpec(memory_space=pl.ANY)
    vmem = pl.BlockSpec(memory_space=pltpu.VMEM)
    sent, grad = pl.pallas_call(
        functools.partial(kernel, (sections, count, cols, chunks, rows, grad_scale)),
        out_shape=[jax.ShapeDtypeStruct((total_rows, width), bf)] + [jax.ShapeDtypeStruct(flat, f32)],
        in_specs=[anywhere] * 3,
        out_specs=[anywhere, vmem],
        scratch_shapes=[
            pltpu.VMEM((chunks, total_rows, cols), bf),
            pltpu.VMEM((chunks, total_rows, cols), bf),
            pltpu.VMEM((chunks, tall, cols), bf),
            pltpu.VMEM((chunks, total_rows, cols), bf),
            pltpu.VMEM((total_rows, 2 * block), f32),
            pltpu.VMEM((total_rows, block), f32),
            pltpu.VMEM((block, total_rows), bf),
            pltpu.VMEM((total_rows, 2 * block), bf),
            pltpu.VMEM((chunks, 2, 2, depth, rows, cols), bf),
            pltpu.VMEM((chunks, 2, depth, rows, cols), bf),
            pltpu.VMEM((chunks, depth, rows, cols), bf),
            pltpu.VMEM((chunks, depth, rows, cols), f32),
            pltpu.VMEM((chunks, depth, rows, cols), bf),
            pltpu.VMEM((chunks, depth, rows, cols), bf),
            pltpu.VMEM((chunks, depth - 1, rows, cols), bf),
            dma((chunks,)), dma((chunks,)), dma((chunks,)), dma((chunks,)),
            dma((chunks,)), dma((chunks,)),
            dma((chunks,)), dma((chunks,)),
            dma((chunks,)), dma((chunks,)),
            dma((depth - 1, chunks)), dma((depth - 1, chunks)),
        ],
        compiler_params=pltpu.CompilerParams(
            collective_id=0, has_side_effects=True, vmem_limit_bytes=60 * 1024 * 1024),
        cost_estimate=pl.CostEstimate(
            flops=12 * total_rows * block * width, bytes_accessed=2 * tall * width + 10 * total_rows * width,
            transcendentals=total_rows * block),
    )(acts.reshape(total_rows, width), out_grad.reshape(total_rows, width), params[0])
    in_grad, nm, ns, up = pl.pallas_call(
        finish_kernel,
        out_shape=[jax.ShapeDtypeStruct((total_rows, width), bf)] + [jax.ShapeDtypeStruct(flat, f32)] * 3,
        in_specs=[anywhere] + [vmem] * 3,
        out_specs=[anywhere] + [vmem] * 3,
        scratch_shapes=[pltpu.SemaphoreType.DMA],
        compiler_params=pltpu.CompilerParams(vmem_limit_bytes=60 * 1024 * 1024),
        cost_estimate=pl.CostEstimate(flops=0, bytes_accessed=4 * total_rows * width, transcendentals=0),
    )(sent, grad, moment.reshape(flat), second.reshape(flat))
    return (in_grad.reshape(acts.shape), nm.reshape(moment.shape), ns.reshape(moment.shape), up.reshape(moment.shape))


def fits(sizes, acts, params):
    count, block = sizes["dp"], params.shape[1] // 3
    micro_rows = acts.shape[1] * acts.shape[2] // count
    return (count % 4 == 0 and count >= 8 and block % (16 * count) == 0 and block % 128 == 0
            and micro_rows % 128 == 0 and acts.shape[2] // count % 16 == 0 and chunk_width(acts.shape[3]) > 0)


def from_behind(value, axis, steps):
    count = lax.axis_size(axis)
    leading, last = (max(0, -steps), min(count, count - steps))
    return lax.ppermute(value, axis, [(source, source + steps) for source in range(leading, last)])


def backward(inputs, grad_rows, weights_in, weights_down):
    block_size = weights_down.shape[0]
    gate_up = lax.dot_general(
        inputs, weights_in, (((1,), (1,)), ((), ())), preferred_element_type=jnp.float32
    )
    gate_values = gate_up[:, :block_size]
    up_values = gate_up[:, block_size:]
    sigmoid_gate = jax.nn.sigmoid(gate_values)
    activated = gate_values * sigmoid_gate
    d_hidden = lax.dot_general(
        grad_rows, weights_down, (((1,), (1,)), ((), ())), preferred_element_type=jnp.float32
    )
    d_gate = d_hidden * up_values * sigmoid_gate * (1.0 + gate_values * (1.0 - sigmoid_gate))
    d_up = d_hidden * activated
    d_gate_up = jnp.concatenate([d_gate, d_up], axis=1).astype(jnp.bfloat16)
    hidden = (activated * up_values).astype(jnp.bfloat16)
    passed = grad_rows.astype(jnp.float32) + jnp.dot(
        d_gate_up, weights_in, preferred_element_type=jnp.float32
    )
    return (passed.astype(jnp.bfloat16), hidden)


def place_slot(stack, value, slot_index, active):
    previous = lax.dynamic_index_in_dim(stack, slot_index, 0, keepdims=False)
    return lax.dynamic_update_index_in_dim(stack, jnp.where(active, value, previous), slot_index, 0)


def weight_terms(hidden, grad_rows):
    lower = lax.dot_general(
        hidden, grad_rows, (((0,), (0,)), ((), ())), preferred_element_type=jnp.float32
    )
    return lower.reshape(-1)


def local(acts, out_grad, params, moment, second):
    sections = lax.axis_size("pipe")
    section_index = lax.axis_index("pipe")
    inputs = acts[0]
    micro_count = inputs.shape[0]
    tok_rows = inputs.shape[1]
    weights = params[0]
    block_size = weights.shape[0] // 3
    weights_in = weights[: 2 * block_size]
    weights_down = weights[2 * block_size :]
    in_grads = jnp.zeros_like(inputs)
    arrived = jnp.zeros_like(inputs)
    hiddens = jnp.zeros((micro_count, tok_rows, block_size), jnp.bfloat16)
    incoming = jnp.zeros_like(inputs[0])
    tick_count = sections + micro_count - 1
    for tick_index in range(tick_count):
        offset = tick_index - (sections - 1) + section_index
        active = jnp.logical_and(offset >= 0, offset < micro_count)
        slot_index = jnp.clip(offset, 0, micro_count - 1)
        current = lax.dynamic_index_in_dim(inputs, slot_index, 0, keepdims=False)
        top_grad = lax.dynamic_index_in_dim(out_grad, slot_index, 0, keepdims=False)
        grad_rows = jnp.where(section_index == sections - 1, top_grad, incoming)

        def working(current=current, grad_rows=grad_rows):
            return backward(current, grad_rows, weights_in, weights_down)

        def resting(current=current):
            return (jnp.zeros_like(current), jnp.zeros((tok_rows, block_size), jnp.bfloat16))

        passed, hidden = lax.cond(active, working, resting)
        in_grads = place_slot(in_grads, passed, slot_index, active)
        arrived = place_slot(arrived, grad_rows, slot_index, active)
        hiddens = place_slot(hiddens, hidden, slot_index, active)
        if tick_index + 1 < tick_count:
            incoming = from_behind(passed, "pipe", -1)
    row_count = micro_count * tok_rows
    term = weight_terms(hiddens.reshape(row_count, block_size), arrived.reshape(row_count, -1))
    summed = lax.psum_scatter(term, "dp", scatter_dimension=0, tiled=True)
    grad_scale = float(row_count * lax.axis_size("dp")) ** (-0.5)
    gradient = summed * grad_scale
    new_moment = 0.9 * moment[0] + 0.1 * gradient
    new_second = 0.999 * second[0] + 0.001 * gradient * gradient
    update = new_moment / (1.0 - 0.9**10) / (jnp.sqrt(new_second / (1.0 - 0.999**10)) + 1e-08)
    return (in_grads[None], new_moment[None], new_second[None], update[None])


def solution(mesh):
    placed = (
        P("pipe", None, "dp", None),
        P(None, "dp", None),
        P("pipe", None, None),
        P("pipe", "dp"),
        P("pipe", "dp"),
    )
    outs = (P("pipe", None, "dp", None), P("pipe", "dp"), P("pipe", "dp"), P("pipe", "dp"))

    def run(acts, out_grad, params, moment, second):
        body = fused if fits(mesh.shape, acts, params) else local
        return jax.shard_map(body, mesh=mesh, in_specs=placed, out_specs=outs, check_vma=False)(
            acts, out_grad, params, moment, second)

    return run
```

```python
import functools

import jax
import jax.numpy as jnp
from jax import lax
from jax.experimental import pallas as pl
from jax.experimental.pallas import tpu as pltpu
from jax.sharding import PartitionSpec as P

MESH = pl.DeviceIdType.MESH
NT = (((1,), (1,)), ((), ()))


def chunk_width(width):
    return max((w for w in (128, 256, 384, 512) if width % w == 0), default=0)


def kernel(dims, x_hbm, g_hbm, w_hbm, out_hbm, grad_ref,
           x, g, w, ig, gu, dh, hid, dgu, part, r1, send2, own, r2, send3, r3,
           load_x, load_g, load_w, store, sy, ry, s1, q1, s2, q2, s3, q3):
    sections, count, cols, chunks, rows, grad_scale = dims
    depth = count // 4
    block = hid.shape[0]
    sec = lax.axis_index("pipe")
    me = lax.axis_index("dp")
    core, xx, zz = lax.rem(me, 2), lax.rem(me // 2, 2), me // 4
    last = sec == sections - 1
    core_peer = me + 1 - 2 * core
    x_peer = me + 2 - 4 * xx
    z_peers = [me + 4 * (lax.rem(zz + j, depth) - zz) for j in range(1, depth)]

    def at(c):
        return pl.ds(pl.multiple_of(c * cols, cols), cols)

    def loads(c):
        return (pltpu.make_async_copy(w_hbm.at[:, at(c)], w.at[c], load_w.at[c]),
                pltpu.make_async_copy(x_hbm.at[:, at(c)], x.at[c], load_x.at[c]))

    def load_grad(c):
        return pltpu.make_async_copy(g_hbm.at[:, at(c)], g.at[c], load_g.at[c])

    def relay(c):
        return pltpu.make_async_remote_copy(
            ig.at[c], g.at[c], sy.at[c], ry.at[c],
            device_id={"pipe": lax.max(sec - 1, 0), "dp": me}, device_id_type=MESH)

    def stage1(c):
        return pltpu.make_async_remote_copy(
            part.at[c, 1 - core], r1.at[c], s1.at[c], q1.at[c],
            device_id={"pipe": sec, "dp": core_peer}, device_id_type=MESH)

    def stage2(c):
        return pltpu.make_async_remote_copy(
            send2.at[c], r2.at[c], s2.at[c], q2.at[c],
            device_id={"pipe": sec, "dp": x_peer}, device_id_type=MESH)

    def stage3(c, j):
        return pltpu.make_async_remote_copy(
            send3.at[c, lax.rem(zz + j + 1, depth)], r3.at[c, j], s3.at[j, c], q3.at[j, c],
            device_id={"pipe": sec, "dp": z_peers[j]}, device_id_type=MESH)

    def result(c):
        return pltpu.make_async_copy(ig.at[c], out_hbm.at[:, at(c)], store.at[c])

    def each(body, low=0, high=chunks):
        def step(c, carry):
            body(c)
            return carry
        lax.fori_loop(low, high, step, 0)

    barrier = pltpu.get_barrier_semaphore()
    for peer in [core_peer, x_peer] + z_peers:
        pl.semaphore_signal(barrier, inc=1, device_id={"pipe": sec, "dp": peer}, device_id_type=MESH)

    @pl.when(sec > 0)
    def _():
        pl.semaphore_signal(barrier, inc=1, device_id={"pipe": lax.max(sec - 1, 0), "dp": me}, device_id_type=MESH)

    @pl.when(jnp.logical_not(last))
    def _():
        pl.semaphore_signal(barrier, inc=1, device_id={"pipe": lax.min(sec + 1, sections - 1), "dp": me}, device_id_type=MESH)

    def begin(c):
        for copy in loads(c):
            copy.start()

        @pl.when(last)
        def _():
            load_grad(c).start()

    each(begin)
    gu[...] = jnp.zeros_like(gu)
    dh[...] = jnp.zeros_like(dh)

    def add_hidden_grad(c):
        dh[...] += lax.dot_general(g[c], w[c, 2 * block:, :], NT, preferred_element_type=jnp.float32)

    def forward(c):
        for copy in loads(c):
            copy.wait()
        gu[...] += lax.dot_general(x[c], w[c, : 2 * block, :], NT, preferred_element_type=jnp.float32)

        @pl.when(last)
        def _():
            load_grad(c).wait()
            add_hidden_grad(c)

    each(forward)
    gate, up = gu[:, :block], gu[:, block:]
    hid[...] = (gate * jax.nn.sigmoid(gate) * up).T.astype(jnp.bfloat16)

    pl.semaphore_wait(barrier, 1 + depth + lax.min(sec, 1) + lax.min(sections - 1 - sec, 1))

    def input_grad():
        gate_v, up_v, d = gu[:, :block], gu[:, block:], dh[...]
        sg = jax.nn.sigmoid(gate_v)
        dgu[:, :block] = (d * up_v * sg * (1.0 + gate_v * (1.0 - sg))).astype(jnp.bfloat16)
        dgu[:, block:] = (d * gate_v * sg).astype(jnp.bfloat16)

        def one(c):
            ig[c] = (g[c].astype(jnp.float32) + jnp.dot(
                dgu[...], w[c, : 2 * block, :], preferred_element_type=jnp.float32)).astype(jnp.bfloat16)

            @pl.when(sec > 0)
            def _():
                relay(c).start()

            result(c).start()

        each(one)

    @pl.when(last)
    def _():
        input_grad()

    def step(t):
        @pl.when(t < chunks)
        def _():
            @pl.when(jnp.logical_not(last))
            def _():
                relay(t).wait_recv()

            term = jnp.dot(hid[...], g[t], preferred_element_type=jnp.float32)
            for owner in range(count):
                part[t, owner % 2, owner // 2 % 2, owner // 4] = term[
                    owner * rows:(owner + 1) * rows].astype(jnp.bfloat16)
            stage1(t).start()

            @pl.when(jnp.logical_not(last))
            def _():
                add_hidden_grad(t)

        @pl.when(jnp.logical_and(t >= 1, t <= chunks))
        def _():
            c = t - 1
            stage1(c).wait_recv()
            for z in range(depth):
                send2[c, z] = (part[c, core, 1 - xx, z].astype(jnp.float32)
                                      + r1[c, 1 - xx, z].astype(jnp.float32)).astype(jnp.bfloat16)
            stage2(c).start()
            for z in range(depth):
                own[c, z] = (part[c, core, xx, z].astype(jnp.float32)
                                    + r1[c, xx, z].astype(jnp.float32))

        @pl.when(jnp.logical_and(t >= 2, t <= chunks + 1))
        def _():
            c = t - 2
            stage2(c).wait_recv()
            for z in range(depth):
                total = own[c, z] + r2[c, z].astype(jnp.float32)
                own[c, z] = total
                send3[c, z] = total.astype(jnp.bfloat16)
            for j in range(depth - 1):
                stage3(c, j).start()

        @pl.when(jnp.logical_and(t == chunks, jnp.logical_not(last)))
        def _():
            input_grad()

        @pl.when(t >= 3)
        def _():
            c = t - 3
            total = own[c, zz]
            for j in range(depth - 1):
                stage3(c, j).wait_recv()
            for j in range(depth - 1):
                total = total + r3[c, j].astype(jnp.float32)
            grad = total * grad_scale
            lanes = cols // 128
            for k in range(lanes):
                where = pl.ds(c * lanes + k, rows, stride=chunks * lanes)
                grad_ref[where, :] = grad[:, k * 128:(k + 1) * 128]

    each(step, 0, chunks + 3)

    def finish(c):
        stage1(c).wait_send()
        stage2(c).wait_send()
        for j in range(depth - 1):
            stage3(c, j).wait_send()

        @pl.when(sec > 0)
        def _():
            relay(c).wait_send()

        result(c).wait()

    each(finish)


def finish_kernel(sent_ref, grad_ref, m_ref, s_ref, out_hbm, nm_hbm, ns_hbm, up_hbm, nm, ns, up, sem):
    pairs = ((sent_ref, out_hbm), (nm, nm_hbm), (ns, ns_hbm), (up, up_hbm))
    copies = [pltpu.make_async_copy(source, target, sem.at[i]) for i, (source, target) in enumerate(pairs)]
    copies[0].start()
    grad = grad_ref[...]
    nm[...] = 0.9 * m_ref[...] + 0.1 * grad
    copies[1].start()
    ns[...] = 0.999 * s_ref[...] + 0.001 * grad * grad
    copies[2].start()
    up[...] = nm[...] / (1.0 - 0.9**10) / (jnp.sqrt(ns[...] / (1.0 - 0.999**10)) + 1e-08)
    copies[3].start()
    for copy in copies:
        copy.wait()


def fused(acts, out_grad, params, moment, second):
    sections, count = lax.axis_size("pipe"), lax.axis_size("dp")
    _, micro, tok, width = acts.shape
    tall = params.shape[1]
    block = tall // 3
    total_rows = micro * tok
    cols = chunk_width(width)
    chunks = width // cols
    rows = block // count
    depth = count // 4
    flat = (rows * width // 128, 128)
    grad_scale = float(total_rows * count) ** (-0.5)
    bf, f32 = jnp.bfloat16, jnp.float32
    dma = pltpu.SemaphoreType.DMA
    anywhere = pl.BlockSpec(memory_space=pl.ANY)
    vmem = pl.BlockSpec(memory_space=pltpu.VMEM)
    hbm = pl.BlockSpec(memory_space=pltpu.HBM)
    sent, grad = pl.pallas_call(
        functools.partial(kernel, (sections, count, cols, chunks, rows, grad_scale)),
        out_shape=[jax.ShapeDtypeStruct((total_rows, width), bf)] + [jax.ShapeDtypeStruct(flat, f32)],
        in_specs=[hbm] * 3,
        out_specs=[anywhere, vmem],
        scratch_shapes=[
            pltpu.VMEM((chunks, total_rows, cols), bf),
            pltpu.VMEM((chunks, total_rows, cols), bf),
            pltpu.VMEM((chunks, tall, cols), bf),
            pltpu.VMEM((chunks, total_rows, cols), bf),
            pltpu.VMEM((total_rows, 2 * block), f32),
            pltpu.VMEM((total_rows, block), f32),
            pltpu.VMEM((block, total_rows), bf),
            pltpu.VMEM((total_rows, 2 * block), bf),
            pltpu.VMEM((chunks, 2, 2, depth, rows, cols), bf),
            pltpu.VMEM((chunks, 2, depth, rows, cols), bf),
            pltpu.VMEM((chunks, depth, rows, cols), bf),
            pltpu.VMEM((chunks, depth, rows, cols), f32),
            pltpu.VMEM((chunks, depth, rows, cols), bf),
            pltpu.VMEM((chunks, depth, rows, cols), bf),
            pltpu.VMEM((chunks, depth - 1, rows, cols), bf),
            dma((chunks,)), dma((chunks,)), dma((chunks,)), dma((chunks,)),
            dma((chunks,)), dma((chunks,)),
            dma((chunks,)), dma((chunks,)),
            dma((chunks,)), dma((chunks,)),
            dma((depth - 1, chunks)), dma((depth - 1, chunks)),
        ],
        compiler_params=pltpu.CompilerParams(
            collective_id=0, has_side_effects=True, vmem_limit_bytes=32 * 1024 * 1024),
        cost_estimate=pl.CostEstimate(
            flops=12 * total_rows * block * width, bytes_accessed=2 * tall * width + 10 * total_rows * width,
            transcendentals=total_rows * block),
    )(acts.reshape(total_rows, width), out_grad.reshape(total_rows, width), params[0])
    in_grad, nm, ns, up = pl.pallas_call(
        finish_kernel,
        out_shape=[jax.ShapeDtypeStruct((total_rows, width), bf)] + [jax.ShapeDtypeStruct(flat, f32)] * 3,
        in_specs=[vmem] * 4,
        out_specs=[hbm] * 4,
        scratch_shapes=[pltpu.VMEM(flat, f32)] * 3 + [dma((4,))],
        compiler_params=pltpu.CompilerParams(vmem_limit_bytes=16 * 1024 * 1024),
        cost_estimate=pl.CostEstimate(flops=0, bytes_accessed=4 * total_rows * width, transcendentals=0),
    )(sent, grad, moment.reshape(flat), second.reshape(flat))
    return (in_grad.reshape(acts.shape), nm.reshape(moment.shape), ns.reshape(moment.shape), up.reshape(moment.shape))


def fits(sizes, acts, params):
    count, block = sizes["dp"], params.shape[1] // 3
    micro_rows = acts.shape[1] * acts.shape[2] // count
    return (count % 4 == 0 and count >= 8 and block % (16 * count) == 0 and block % 128 == 0
            and micro_rows % 128 == 0 and acts.shape[2] // count % 16 == 0 and chunk_width(acts.shape[3]) > 0)


def from_behind(value, axis, steps):
    count = lax.axis_size(axis)
    leading, last = (max(0, -steps), min(count, count - steps))
    return lax.ppermute(value, axis, [(source, source + steps) for source in range(leading, last)])


def backward(inputs, grad_rows, weights_in, weights_down):
    block_size = weights_down.shape[0]
    gate_up = lax.dot_general(
        inputs, weights_in, (((1,), (1,)), ((), ())), preferred_element_type=jnp.float32
    )
    gate_values = gate_up[:, :block_size]
    up_values = gate_up[:, block_size:]
    sigmoid_gate = jax.nn.sigmoid(gate_values)
    activated = gate_values * sigmoid_gate
    d_hidden = lax.dot_general(
        grad_rows, weights_down, (((1,), (1,)), ((), ())), preferred_element_type=jnp.float32
    )
    d_gate = d_hidden * up_values * sigmoid_gate * (1.0 + gate_values * (1.0 - sigmoid_gate))
    d_up = d_hidden * activated
    d_gate_up = jnp.concatenate([d_gate, d_up], axis=1).astype(jnp.bfloat16)
    hidden = (activated * up_values).astype(jnp.bfloat16)
    passed = grad_rows.astype(jnp.float32) + jnp.dot(
        d_gate_up, weights_in, preferred_element_type=jnp.float32
    )
    return (passed.astype(jnp.bfloat16), hidden)


def place_slot(stack, value, slot_index, active):
    previous = lax.dynamic_index_in_dim(stack, slot_index, 0, keepdims=False)
    return lax.dynamic_update_index_in_dim(stack, jnp.where(active, value, previous), slot_index, 0)


def weight_terms(hidden, grad_rows):
    lower = lax.dot_general(
        hidden, grad_rows, (((0,), (0,)), ((), ())), preferred_element_type=jnp.float32
    )
    return lower.reshape(-1)


def local(acts, out_grad, params, moment, second):
    sections = lax.axis_size("pipe")
    section_index = lax.axis_index("pipe")
    inputs = acts[0]
    micro_count = inputs.shape[0]
    tok_rows = inputs.shape[1]
    weights = params[0]
    block_size = weights.shape[0] // 3
    weights_in = weights[: 2 * block_size]
    weights_down = weights[2 * block_size :]
    in_grads = jnp.zeros_like(inputs)
    arrived = jnp.zeros_like(inputs)
    hiddens = jnp.zeros((micro_count, tok_rows, block_size), jnp.bfloat16)
    incoming = jnp.zeros_like(inputs[0])
    tick_count = sections + micro_count - 1
    for tick_index in range(tick_count):
        offset = tick_index - (sections - 1) + section_index
        active = jnp.logical_and(offset >= 0, offset < micro_count)
        slot_index = jnp.clip(offset, 0, micro_count - 1)
        current = lax.dynamic_index_in_dim(inputs, slot_index, 0, keepdims=False)
        top_grad = lax.dynamic_index_in_dim(out_grad, slot_index, 0, keepdims=False)
        grad_rows = jnp.where(section_index == sections - 1, top_grad, incoming)

        def working(current=current, grad_rows=grad_rows):
            return backward(current, grad_rows, weights_in, weights_down)

        def resting(current=current):
            return (jnp.zeros_like(current), jnp.zeros((tok_rows, block_size), jnp.bfloat16))

        passed, hidden = lax.cond(active, working, resting)
        in_grads = place_slot(in_grads, passed, slot_index, active)
        arrived = place_slot(arrived, grad_rows, slot_index, active)
        hiddens = place_slot(hiddens, hidden, slot_index, active)
        if tick_index + 1 < tick_count:
            incoming = from_behind(passed, "pipe", -1)
    row_count = micro_count * tok_rows
    term = weight_terms(hiddens.reshape(row_count, block_size), arrived.reshape(row_count, -1))
    summed = lax.psum_scatter(term, "dp", scatter_dimension=0, tiled=True)
    grad_scale = float(row_count * lax.axis_size("dp")) ** (-0.5)
    gradient = summed * grad_scale
    new_moment = 0.9 * moment[0] + 0.1 * gradient
    new_second = 0.999 * second[0] + 0.001 * gradient * gradient
    update = new_moment / (1.0 - 0.9**10) / (jnp.sqrt(new_second / (1.0 - 0.999**10)) + 1e-08)
    return (in_grads[None], new_moment[None], new_second[None], update[None])


def solution(mesh):
    placed = (
        P("pipe", None, "dp", None),
        P(None, "dp", None),
        P("pipe", None, None),
        P("pipe", "dp"),
        P("pipe", "dp"),
    )
    outs = (P("pipe", None, "dp", None), P("pipe", "dp"), P("pipe", "dp"), P("pipe", "dp"))

    def run(acts, out_grad, params, moment, second):
        body = fused if fits(mesh.shape, acts, params) else local
        return jax.shard_map(body, mesh=mesh, in_specs=placed, out_specs=outs, check_vma=False)(
            acts, out_grad, params, moment, second)

    return run
```

```python
import functools

import jax
import jax.numpy as jnp
from jax import lax
from jax.experimental import pallas as pl
from jax.experimental.pallas import tpu as pltpu
from jax.sharding import PartitionSpec as P

MESH = pl.DeviceIdType.MESH
NT = (((1,), (1,)), ((), ()))


def chunk_width(width):
    return max((w for w in (128, 256, 384, 512) if width % w == 0), default=0)


def kernel(dims, x_hbm, g_hbm, w_hbm, out_hbm, grad_ref,
           x, g, w, ig, gu, dh, hid, dgu, part, r1, send2, own, r2, send3, r3,
           load_x, load_g, load_w, store, sy, ry, s1, q1, s2, q2, s3, q3):
    sections, count, cols, chunks, rows, grad_scale = dims
    depth = count // 4
    block = hid.shape[0]
    sec = lax.axis_index("pipe")
    me = lax.axis_index("dp")
    core, xx, zz = lax.rem(me, 2), lax.rem(me // 2, 2), me // 4
    last = sec == sections - 1
    core_peer = me + 1 - 2 * core
    x_peer = me + 2 - 4 * xx
    z_peers = [me + 4 * (lax.rem(zz + j, depth) - zz) for j in range(1, depth)]

    def at(c):
        return pl.ds(pl.multiple_of(c * cols, cols), cols)

    def loads(c):
        return (pltpu.make_async_copy(w_hbm.at[:, at(c)], w.at[c], load_w.at[c]),
                pltpu.make_async_copy(x_hbm.at[:, at(c)], x.at[c], load_x.at[c]))

    def load_grad(c):
        return pltpu.make_async_copy(g_hbm.at[:, at(c)], g.at[c], load_g.at[c])

    def relay(c):
        return pltpu.make_async_remote_copy(
            ig.at[c], g.at[c], sy.at[c], ry.at[c],
            device_id={"pipe": lax.max(sec - 1, 0), "dp": me}, device_id_type=MESH)

    def stage1(c):
        return pltpu.make_async_remote_copy(
            part.at[c, 1 - core], r1.at[c], s1.at[c], q1.at[c],
            device_id={"pipe": sec, "dp": core_peer}, device_id_type=MESH)

    def stage2(c):
        return pltpu.make_async_remote_copy(
            send2.at[c], r2.at[c], s2.at[c], q2.at[c],
            device_id={"pipe": sec, "dp": x_peer}, device_id_type=MESH)

    def stage3(c, j):
        return pltpu.make_async_remote_copy(
            send3.at[c, lax.rem(zz + j + 1, depth)], r3.at[c, j], s3.at[j, c], q3.at[j, c],
            device_id={"pipe": sec, "dp": z_peers[j]}, device_id_type=MESH)

    def result(c):
        return pltpu.make_async_copy(ig.at[c], out_hbm.at[:, at(c)], store.at[c])

    def each(body, low=0, high=chunks):
        def step(c, carry):
            body(c)
            return carry
        lax.fori_loop(low, high, step, 0)

    barrier = pltpu.get_barrier_semaphore()
    for peer in [core_peer, x_peer] + z_peers:
        pl.semaphore_signal(barrier, inc=1, device_id={"pipe": sec, "dp": peer}, device_id_type=MESH)

    @pl.when(sec > 0)
    def _():
        pl.semaphore_signal(barrier, inc=1, device_id={"pipe": lax.max(sec - 1, 0), "dp": me}, device_id_type=MESH)

    @pl.when(jnp.logical_not(last))
    def _():
        pl.semaphore_signal(barrier, inc=1, device_id={"pipe": lax.min(sec + 1, sections - 1), "dp": me}, device_id_type=MESH)

    def begin(c):
        for copy in loads(c):
            copy.start()

        @pl.when(last)
        def _():
            load_grad(c).start()

    each(begin)
    gu[...] = jnp.zeros_like(gu)
    dh[...] = jnp.zeros_like(dh)

    def add_hidden_grad(c):
        dh[...] += lax.dot_general(g[c], w[c, 2 * block:, :], NT, preferred_element_type=jnp.float32)

    def forward(c):
        for copy in loads(c):
            copy.wait()
        gu[...] += lax.dot_general(x[c], w[c, : 2 * block, :], NT, preferred_element_type=jnp.float32)

        @pl.when(last)
        def _():
            load_grad(c).wait()
            add_hidden_grad(c)

    each(forward)
    gate, up = gu[:, :block], gu[:, block:]
    hid[...] = (gate * jax.nn.sigmoid(gate) * up).T.astype(jnp.bfloat16)

    pl.semaphore_wait(barrier, 1 + depth + lax.min(sec, 1) + lax.min(sections - 1 - sec, 1))

    def input_grad():
        gate_v, up_v, d = gu[:, :block], gu[:, block:], dh[...]
        sg = jax.nn.sigmoid(gate_v)
        dgu[:, :block] = (d * up_v * sg * (1.0 + gate_v * (1.0 - sg))).astype(jnp.bfloat16)
        dgu[:, block:] = (d * gate_v * sg).astype(jnp.bfloat16)

        def one(c):
            ig[c] = (g[c].astype(jnp.float32) + jnp.dot(
                dgu[...], w[c, : 2 * block, :], preferred_element_type=jnp.float32)).astype(jnp.bfloat16)

            @pl.when(sec > 0)
            def _():
                relay(c).start()

            result(c).start()

        each(one)

    @pl.when(last)
    def _():
        input_grad()

    def step(t):
        @pl.when(t < chunks)
        def _():
            @pl.when(jnp.logical_not(last))
            def _():
                relay(t).wait_recv()

            term = jnp.dot(hid[...], g[t], preferred_element_type=jnp.float32)
            for owner in range(count):
                part[t, owner % 2, owner // 2 % 2, owner // 4] = term[
                    owner * rows:(owner + 1) * rows].astype(jnp.bfloat16)
            stage1(t).start()

            @pl.when(jnp.logical_not(last))
            def _():
                add_hidden_grad(t)

        @pl.when(jnp.logical_and(t >= 1, t <= chunks))
        def _():
            c = t - 1
            stage1(c).wait_recv()
            for z in range(depth):
                send2[c, z] = (part[c, core, 1 - xx, z].astype(jnp.float32)
                                      + r1[c, 1 - xx, z].astype(jnp.float32)).astype(jnp.bfloat16)
            stage2(c).start()
            for z in range(depth):
                own[c, z] = (part[c, core, xx, z].astype(jnp.float32)
                                    + r1[c, xx, z].astype(jnp.float32))

        @pl.when(jnp.logical_and(t >= 2, t <= chunks + 1))
        def _():
            c = t - 2
            stage2(c).wait_recv()
            for z in range(depth):
                total = own[c, z] + r2[c, z].astype(jnp.float32)
                own[c, z] = total
                send3[c, z] = total.astype(jnp.bfloat16)
            for j in range(depth - 1):
                stage3(c, j).start()

        @pl.when(jnp.logical_and(t == chunks, jnp.logical_not(last)))
        def _():
            input_grad()

        @pl.when(t >= 3)
        def _():
            c = t - 3
            total = own[c, zz]
            for j in range(depth - 1):
                stage3(c, j).wait_recv()
            for j in range(depth - 1):
                total = total + r3[c, j].astype(jnp.float32)
            grad = total * grad_scale
            lanes = cols // 128
            for k in range(lanes):
                where = pl.ds(c * lanes + k, rows, stride=chunks * lanes)
                grad_ref[where, :] = grad[:, k * 128:(k + 1) * 128]

    each(step, 0, chunks + 3)

    def finish(c):
        stage1(c).wait_send()
        stage2(c).wait_send()
        for j in range(depth - 1):
            stage3(c, j).wait_send()

        @pl.when(sec > 0)
        def _():
            relay(c).wait_send()

        result(c).wait()

    each(finish)


def finish_kernel(sent_ref, grad_ref, m_ref, s_ref, out_hbm, nm_hbm, ns_hbm, up_hbm, nm, ns, up, sem):
    pairs = ((sent_ref, out_hbm), (nm, nm_hbm), (ns, ns_hbm), (up, up_hbm))
    copies = [pltpu.make_async_copy(source, target, sem.at[i]) for i, (source, target) in enumerate(pairs)]
    copies[0].start()
    grad = grad_ref[...]
    nm[...] = 0.9 * m_ref[...] + 0.1 * grad
    copies[1].start()
    ns[...] = 0.999 * s_ref[...] + 0.001 * grad * grad
    copies[2].start()
    up[...] = nm[...] / (1.0 - 0.9**10) / (jnp.sqrt(ns[...] / (1.0 - 0.999**10)) + 1e-08)
    copies[3].start()
    for copy in copies:
        copy.wait()


def fused(acts, out_grad, params, moment, second):
    sections, count = lax.axis_size("pipe"), lax.axis_size("dp")
    _, micro, tok, width = acts.shape
    tall = params.shape[1]
    block = tall // 3
    total_rows = micro * tok
    cols = chunk_width(width)
    chunks = width // cols
    rows = block // count
    depth = count // 4
    flat = (rows * width // 128, 128)
    grad_scale = float(total_rows * count) ** (-0.5)
    bf, f32 = jnp.bfloat16, jnp.float32
    dma = pltpu.SemaphoreType.DMA
    anywhere = pl.BlockSpec(memory_space=pl.ANY)
    vmem = pl.BlockSpec(memory_space=pltpu.VMEM)
    hbm = pl.BlockSpec(memory_space=pltpu.HBM)
    sent, grad = pl.pallas_call(
        functools.partial(kernel, (sections, count, cols, chunks, rows, grad_scale)),
        out_shape=[jax.ShapeDtypeStruct((total_rows, width), bf)] + [jax.ShapeDtypeStruct(flat, f32)],
        in_specs=[hbm] * 3,
        out_specs=[anywhere, vmem],
        scratch_shapes=[
            pltpu.VMEM((chunks, total_rows, cols), bf),
            pltpu.VMEM((chunks, total_rows, cols), bf),
            pltpu.VMEM((chunks, tall, cols), bf),
            pltpu.VMEM((chunks, total_rows, cols), bf),
            pltpu.VMEM((total_rows, 2 * block), f32),
            pltpu.VMEM((total_rows, block), f32),
            pltpu.VMEM((block, total_rows), bf),
            pltpu.VMEM((total_rows, 2 * block), bf),
            pltpu.VMEM((chunks, 2, 2, depth, rows, cols), bf),
            pltpu.VMEM((chunks, 2, depth, rows, cols), bf),
            pltpu.VMEM((chunks, depth, rows, cols), bf),
            pltpu.VMEM((chunks, depth, rows, cols), f32),
            pltpu.VMEM((chunks, depth, rows, cols), bf),
            pltpu.VMEM((chunks, depth, rows, cols), bf),
            pltpu.VMEM((chunks, depth - 1, rows, cols), bf),
            dma((chunks,)), dma((chunks,)), dma((chunks,)), dma((chunks,)),
            dma((chunks,)), dma((chunks,)),
            dma((chunks,)), dma((chunks,)),
            dma((chunks,)), dma((chunks,)),
            dma((depth - 1, chunks)), dma((depth - 1, chunks)),
        ],
        compiler_params=pltpu.CompilerParams(
            collective_id=0, has_side_effects=True, vmem_limit_bytes=60 * 1024 * 1024),
        cost_estimate=pl.CostEstimate(
            flops=12 * total_rows * block * width, bytes_accessed=2 * tall * width + 10 * total_rows * width,
            transcendentals=total_rows * block),
    )(acts.reshape(total_rows, width), out_grad.reshape(total_rows, width), params[0])
    in_grad, nm, ns, up = pl.pallas_call(
        finish_kernel,
        out_shape=[jax.ShapeDtypeStruct((total_rows, width), bf)] + [jax.ShapeDtypeStruct(flat, f32)] * 3,
        in_specs=[vmem] * 4,
        out_specs=[hbm] * 4,
        scratch_shapes=[pltpu.VMEM(flat, f32)] * 3 + [dma((4,))],
        compiler_params=pltpu.CompilerParams(vmem_limit_bytes=60 * 1024 * 1024),
        cost_estimate=pl.CostEstimate(flops=0, bytes_accessed=4 * total_rows * width, transcendentals=0),
    )(sent, grad, moment.reshape(flat), second.reshape(flat))
    return (in_grad.reshape(acts.shape), nm.reshape(moment.shape), ns.reshape(moment.shape), up.reshape(moment.shape))


def fits(sizes, acts, params):
    count, block = sizes["dp"], params.shape[1] // 3
    micro_rows = acts.shape[1] * acts.shape[2] // count
    return (count % 4 == 0 and count >= 8 and block % (16 * count) == 0 and block % 128 == 0
            and micro_rows % 128 == 0 and acts.shape[2] // count % 16 == 0 and chunk_width(acts.shape[3]) > 0)


def from_behind(value, axis, steps):
    count = lax.axis_size(axis)
    leading, last = (max(0, -steps), min(count, count - steps))
    return lax.ppermute(value, axis, [(source, source + steps) for source in range(leading, last)])


def backward(inputs, grad_rows, weights_in, weights_down):
    block_size = weights_down.shape[0]
    gate_up = lax.dot_general(
        inputs, weights_in, (((1,), (1,)), ((), ())), preferred_element_type=jnp.float32
    )
    gate_values = gate_up[:, :block_size]
    up_values = gate_up[:, block_size:]
    sigmoid_gate = jax.nn.sigmoid(gate_values)
    activated = gate_values * sigmoid_gate
    d_hidden = lax.dot_general(
        grad_rows, weights_down, (((1,), (1,)), ((), ())), preferred_element_type=jnp.float32
    )
    d_gate = d_hidden * up_values * sigmoid_gate * (1.0 + gate_values * (1.0 - sigmoid_gate))
    d_up = d_hidden * activated
    d_gate_up = jnp.concatenate([d_gate, d_up], axis=1).astype(jnp.bfloat16)
    hidden = (activated * up_values).astype(jnp.bfloat16)
    passed = grad_rows.astype(jnp.float32) + jnp.dot(
        d_gate_up, weights_in, preferred_element_type=jnp.float32
    )
    return (passed.astype(jnp.bfloat16), hidden)


def place_slot(stack, value, slot_index, active):
    previous = lax.dynamic_index_in_dim(stack, slot_index, 0, keepdims=False)
    return lax.dynamic_update_index_in_dim(stack, jnp.where(active, value, previous), slot_index, 0)


def weight_terms(hidden, grad_rows):
    lower = lax.dot_general(
        hidden, grad_rows, (((0,), (0,)), ((), ())), preferred_element_type=jnp.float32
    )
    return lower.reshape(-1)


def local(acts, out_grad, params, moment, second):
    sections = lax.axis_size("pipe")
    section_index = lax.axis_index("pipe")
    inputs = acts[0]
    micro_count = inputs.shape[0]
    tok_rows = inputs.shape[1]
    weights = params[0]
    block_size = weights.shape[0] // 3
    weights_in = weights[: 2 * block_size]
    weights_down = weights[2 * block_size :]
    in_grads = jnp.zeros_like(inputs)
    arrived = jnp.zeros_like(inputs)
    hiddens = jnp.zeros((micro_count, tok_rows, block_size), jnp.bfloat16)
    incoming = jnp.zeros_like(inputs[0])
    tick_count = sections + micro_count - 1
    for tick_index in range(tick_count):
        offset = tick_index - (sections - 1) + section_index
        active = jnp.logical_and(offset >= 0, offset < micro_count)
        slot_index = jnp.clip(offset, 0, micro_count - 1)
        current = lax.dynamic_index_in_dim(inputs, slot_index, 0, keepdims=False)
        top_grad = lax.dynamic_index_in_dim(out_grad, slot_index, 0, keepdims=False)
        grad_rows = jnp.where(section_index == sections - 1, top_grad, incoming)

        def working(current=current, grad_rows=grad_rows):
            return backward(current, grad_rows, weights_in, weights_down)

        def resting(current=current):
            return (jnp.zeros_like(current), jnp.zeros((tok_rows, block_size), jnp.bfloat16))

        passed, hidden = lax.cond(active, working, resting)
        in_grads = place_slot(in_grads, passed, slot_index, active)
        arrived = place_slot(arrived, grad_rows, slot_index, active)
        hiddens = place_slot(hiddens, hidden, slot_index, active)
        if tick_index + 1 < tick_count:
            incoming = from_behind(passed, "pipe", -1)
    row_count = micro_count * tok_rows
    term = weight_terms(hiddens.reshape(row_count, block_size), arrived.reshape(row_count, -1))
    summed = lax.psum_scatter(term, "dp", scatter_dimension=0, tiled=True)
    grad_scale = float(row_count * lax.axis_size("dp")) ** (-0.5)
    gradient = summed * grad_scale
    new_moment = 0.9 * moment[0] + 0.1 * gradient
    new_second = 0.999 * second[0] + 0.001 * gradient * gradient
    update = new_moment / (1.0 - 0.9**10) / (jnp.sqrt(new_second / (1.0 - 0.999**10)) + 1e-08)
    return (in_grads[None], new_moment[None], new_second[None], update[None])


def solution(mesh):
    placed = (
        P("pipe", None, "dp", None),
        P(None, "dp", None),
        P("pipe", None, None),
        P("pipe", "dp"),
        P("pipe", "dp"),
    )
    outs = (P("pipe", None, "dp", None), P("pipe", "dp"), P("pipe", "dp"), P("pipe", "dp"))

    def run(acts, out_grad, params, moment, second):
        body = fused if fits(mesh.shape, acts, params) else local
        return jax.shard_map(body, mesh=mesh, in_specs=placed, out_specs=outs, check_vma=False)(
            acts, out_grad, params, moment, second)

    return run
```

```python
import functools

import jax
import jax.numpy as jnp
from jax import lax
from jax.experimental import pallas as pl
from jax.experimental.pallas import tpu as pltpu
from jax.sharding import PartitionSpec as P

MESH = pl.DeviceIdType.MESH
NT = (((1,), (1,)), ((), ()))


def chunk_width(width):
    return max((w for w in (128, 256, 384, 512) if width % w == 0), default=0)


def kernel(dims, x_hbm, g_hbm, w_hbm, out_hbm, grad_ref,
           x, g, w, ig, gu, dh, hid, dgu, part, r1, send2, own, r2, send3, r3,
           load_x, load_g, load_w, store, sy, ry, s1, q1, s2, q2, s3, q3,
           wa, dgi, sd, qd, sa, qa, sz, qz, sx, qx, sc, qc):
    sections, count, cols, chunks, rows, grad_scale, helped, first = dims
    depth = count // 4
    block = hid.shape[0]
    sec = lax.axis_index("pipe")
    me = lax.axis_index("dp")
    core, xx, zz = lax.rem(me, 2), lax.rem(me // 2, 2), me // 4
    last = sec == sections - 1
    core_peer = me + 1 - 2 * core
    x_peer = me + 2 - 4 * xx
    z_peers = [me + 4 * (lax.rem(zz + j, depth) - zz) for j in range(1, depth)]

    def at(c):
        return pl.ds(pl.multiple_of(c * cols, cols), cols)

    def loads(c):
        return (pltpu.make_async_copy(w_hbm.at[:, at(c)], w.at[c], load_w.at[c]),
                pltpu.make_async_copy(x_hbm.at[:, at(c)], x.at[c], load_x.at[c]))

    def load_grad(c):
        return pltpu.make_async_copy(g_hbm.at[:, at(c)], g.at[c], load_g.at[c])

    def relay(c):
        return pltpu.make_async_remote_copy(
            ig.at[c], g.at[c], sy.at[c], ry.at[c],
            device_id={"pipe": lax.max(sec - 1, 0), "dp": me}, device_id_type=MESH)

    def stage1(c):
        return pltpu.make_async_remote_copy(
            part.at[c, 1 - core], r1.at[c], s1.at[c], q1.at[c],
            device_id={"pipe": sec, "dp": core_peer}, device_id_type=MESH)

    def stage2(c):
        return pltpu.make_async_remote_copy(
            send2.at[c], r2.at[c], s2.at[c], q2.at[c],
            device_id={"pipe": sec, "dp": x_peer}, device_id_type=MESH)

    def stage3(c, j):
        return pltpu.make_async_remote_copy(
            send3.at[c, lax.rem(zz + j + 1, depth)], r3.at[c, j], s3.at[j, c], q3.at[j, c],
            device_id={"pipe": sec, "dp": z_peers[j]}, device_id_type=MESH)

    share = 2 * block // count
    slot = (core * 2 + xx) * depth + zz
    below = {"pipe": lax.max(sec - 1, 0), "dp": me}

    def order(i):
        return lax.rem(i + first, chunks)

    def send_share(a):
        return pltpu.make_async_remote_copy(
            w.at[first + a, pl.ds(pl.multiple_of(slot * share, share), share)], wa.at[a, core, xx, zz],
            sa.at[a], qa.at[a], device_id=below, device_id_type=MESH)

    def send_terms():
        return pltpu.make_async_remote_copy(
            dgu, dgi, sd.at[0], qd.at[0], device_id=below, device_id_type=MESH)

    def gather_z(a, j):
        return pltpu.make_async_remote_copy(
            wa.at[a, core, xx, zz], wa.at[a, core, xx, zz], sz.at[j, a], qz.at[j, a],
            device_id={"pipe": sec, "dp": z_peers[j]}, device_id_type=MESH)

    def gather_x(a):
        return pltpu.make_async_remote_copy(
            wa.at[a, core, xx], wa.at[a, core, xx], sx.at[a], qx.at[a],
            device_id={"pipe": sec, "dp": x_peer}, device_id_type=MESH)

    def gather_core(a):
        return pltpu.make_async_remote_copy(
            wa.at[a, core], wa.at[a, core], sc.at[a], qc.at[a],
            device_id={"pipe": sec, "dp": core_peer}, device_id_type=MESH)

    def is_helped(c):
        return jnp.logical_and(c >= first, c < first + helped)

    def result(c):
        return pltpu.make_async_copy(ig.at[c], out_hbm.at[:, at(c)], store.at[c])

    def each(body, low=0, high=chunks):
        def step(c, carry):
            body(c)
            return carry
        lax.fori_loop(low, high, step, 0)

    barrier = pltpu.get_barrier_semaphore()
    for peer in [core_peer, x_peer] + z_peers:
        pl.semaphore_signal(barrier, inc=1, device_id={"pipe": sec, "dp": peer}, device_id_type=MESH)

    @pl.when(sec > 0)
    def _():
        pl.semaphore_signal(barrier, inc=1, device_id={"pipe": lax.max(sec - 1, 0), "dp": me}, device_id_type=MESH)

    @pl.when(jnp.logical_not(last))
    def _():
        pl.semaphore_signal(barrier, inc=1, device_id={"pipe": lax.min(sec + 1, sections - 1), "dp": me}, device_id_type=MESH)

    def begin(i):
        c = order(i)
        for copy in loads(c):
            copy.start()

        @pl.when(jnp.logical_or(last, is_helped(c)))
        def _():
            load_grad(c).start()

    each(begin)
    gu[...] = jnp.zeros_like(gu)
    dh[...] = jnp.zeros_like(dh)

    def add_hidden_grad(c):
        dh[...] += lax.dot_general(g[c], w[c, 2 * block:, :], NT, preferred_element_type=jnp.float32)

    def forward(i):
        c = order(i)
        for copy in loads(c):
            copy.wait()
        gu[...] += lax.dot_general(x[c], w[c, : 2 * block, :], NT, preferred_element_type=jnp.float32)

        @pl.when(last)
        def _():
            load_grad(c).wait()
            add_hidden_grad(c)

    each(forward, 0, helped)
    pl.semaphore_wait(barrier, 1 + depth + lax.min(sec, 1) + lax.min(sections - 1 - sec, 1))

    @pl.when(sec > 0)
    def _():
        each(lambda a: send_share(a).start(), 0, helped)

    each(forward, helped, chunks)
    gate, up = gu[:, :block], gu[:, block:]
    hid[...] = (gate * jax.nn.sigmoid(gate) * up).T.astype(jnp.bfloat16)

    @pl.when(jnp.logical_not(last))
    def _():
        def spread(a):
            send_share(a).wait_recv()
            for j in range(depth - 1):
                gather_z(a, j).start()

        each(spread, 0, helped)

    def input_grad():
        gate_v, up_v, d = gu[:, :block], gu[:, block:], dh[...]
        sg = jax.nn.sigmoid(gate_v)
        dgu[:, :block] = (d * up_v * sg * (1.0 + gate_v * (1.0 - sg))).astype(jnp.bfloat16)
        dgu[:, block:] = (d * gate_v * sg).astype(jnp.bfloat16)

        @pl.when(sec > 0)
        def _():
            send_terms().start()

        def one(c):
            ig[c] = (g[c].astype(jnp.float32) + jnp.dot(
                dgu[...], w[c, : 2 * block, :], preferred_element_type=jnp.float32)).astype(jnp.bfloat16)

            @pl.when(jnp.logical_and(sec > 0, jnp.logical_not(is_helped(c))))
            def _():
                relay(c).start()

            result(c).start()

        each(one, 0, first)
        each(one, first + helped, chunks)
        each(one, first, first + helped)

    @pl.when(last)
    def _():
        input_grad()

    def step(t):
        @pl.when(t < chunks)
        def _():
            receives = jnp.logical_not(last)

            @pl.when(jnp.logical_and(receives, t < helped))
            def _():
                for j in range(depth - 1):
                    gather_z(t, j).wait_recv()
                gather_x(t).start()

            @pl.when(jnp.logical_and(receives, jnp.logical_and(t >= 1, t <= helped)))
            def _():
                gather_x(t - 1).wait_recv()
                gather_core(t - 1).start()

            @pl.when(jnp.logical_and(receives, t == first))
            def _():
                send_terms().wait_recv()

            @pl.when(jnp.logical_and(receives, is_helped(t)))
            def _():
                a = t - first
                load_grad(t).wait()
                gather_core(a).wait_recv()
                total = g[t].astype(jnp.float32)
                for k in range(2):
                    total = total + jnp.dot(
                        dgi[:, k * block:(k + 1) * block], wa[a, k].reshape(block, cols),
                        preferred_element_type=jnp.float32)
                g[t] = total.astype(jnp.bfloat16)

            @pl.when(jnp.logical_and(receives, jnp.logical_not(is_helped(t))))
            def _():
                relay(t).wait_recv()

            term = jnp.dot(hid[...], g[t], preferred_element_type=jnp.float32)
            for owner in range(count):
                part[t, owner % 2, owner // 2 % 2, owner // 4] = term[
                    owner * rows:(owner + 1) * rows].astype(jnp.bfloat16)
            stage1(t).start()

            @pl.when(jnp.logical_not(last))
            def _():
                add_hidden_grad(t)

        @pl.when(jnp.logical_and(t >= 1, t <= chunks))
        def _():
            c = t - 1
            stage1(c).wait_recv()
            for z in range(depth):
                send2[c, z] = (part[c, core, 1 - xx, z].astype(jnp.float32)
                                      + r1[c, 1 - xx, z].astype(jnp.float32)).astype(jnp.bfloat16)
            stage2(c).start()
            for z in range(depth):
                own[c, z] = (part[c, core, xx, z].astype(jnp.float32)
                                    + r1[c, xx, z].astype(jnp.float32))

        @pl.when(jnp.logical_and(t >= 2, t <= chunks + 1))
        def _():
            c = t - 2
            stage2(c).wait_recv()
            for z in range(depth):
                total = own[c, z] + r2[c, z].astype(jnp.float32)
                own[c, z] = total
                send3[c, z] = total.astype(jnp.bfloat16)
            for j in range(depth - 1):
                stage3(c, j).start()

        @pl.when(jnp.logical_and(t == chunks, jnp.logical_not(last)))
        def _():
            input_grad()

        @pl.when(t >= 3)
        def _():
            c = t - 3
            total = own[c, zz]
            for j in range(depth - 1):
                stage3(c, j).wait_recv()
            for j in range(depth - 1):
                total = total + r3[c, j].astype(jnp.float32)
            grad = total * grad_scale
            lanes = cols // 128
            for k in range(lanes):
                where = pl.ds(c * lanes + k, rows, stride=chunks * lanes)
                grad_ref[where, :] = grad[:, k * 128:(k + 1) * 128]

    each(step, 0, chunks + 3)

    def finish(c):
        stage1(c).wait_send()
        stage2(c).wait_send()
        for j in range(depth - 1):
            stage3(c, j).wait_send()

        @pl.when(jnp.logical_and(sec > 0, jnp.logical_not(is_helped(c))))
        def _():
            relay(c).wait_send()

        result(c).wait()

    each(finish)

    @pl.when(sec > 0)
    def _():
        send_terms().wait_send()
        each(lambda a: send_share(a).wait_send(), 0, helped)

    @pl.when(jnp.logical_not(last))
    def _():
        def finish_gather(a):
            for j in range(depth - 1):
                gather_z(a, j).wait_send()
            gather_x(a).wait_send()
            gather_core(a).wait_send()

        each(finish_gather, 0, helped)


def finish_kernel(sent_ref, grad_ref, m_ref, s_ref, out_hbm, nm_hbm, ns_hbm, up_hbm, nm, ns, up, sem):
    pairs = ((sent_ref, out_hbm), (nm, nm_hbm), (ns, ns_hbm), (up, up_hbm))
    copies = [pltpu.make_async_copy(source, target, sem.at[i]) for i, (source, target) in enumerate(pairs)]
    copies[0].start()
    grad = grad_ref[...]
    nm[...] = 0.9 * m_ref[...] + 0.1 * grad
    copies[1].start()
    ns[...] = 0.999 * s_ref[...] + 0.001 * grad * grad
    copies[2].start()
    up[...] = nm[...] / (1.0 - 0.9**10) / (jnp.sqrt(ns[...] / (1.0 - 0.999**10)) + 1e-08)
    copies[3].start()
    for copy in copies:
        copy.wait()


def fused(acts, out_grad, params, moment, second):
    sections, count = lax.axis_size("pipe"), lax.axis_size("dp")
    _, micro, tok, width = acts.shape
    tall = params.shape[1]
    block = tall // 3
    total_rows = micro * tok
    cols = chunk_width(width)
    chunks = width // cols
    rows = block // count
    depth = count // 4
    helped = chunks * 4 // 11
    first = (chunks - helped + 1) // 2
    share = 2 * block // count
    flat = (rows * width // 128, 128)
    grad_scale = float(total_rows * count) ** (-0.5)
    bf, f32 = jnp.bfloat16, jnp.float32
    dma = pltpu.SemaphoreType.DMA
    anywhere = pl.BlockSpec(memory_space=pl.ANY)
    vmem = pl.BlockSpec(memory_space=pltpu.VMEM)
    hbm = pl.BlockSpec(memory_space=pltpu.HBM)
    sent, grad = pl.pallas_call(
        functools.partial(kernel, (sections, count, cols, chunks, rows, grad_scale, helped, first)),
        out_shape=[jax.ShapeDtypeStruct((total_rows, width), bf)] + [jax.ShapeDtypeStruct(flat, f32)],
        in_specs=[hbm] * 3,
        out_specs=[anywhere, vmem],
        scratch_shapes=[
            pltpu.VMEM((chunks, total_rows, cols), bf),
            pltpu.VMEM((chunks, total_rows, cols), bf),
            pltpu.VMEM((chunks, tall, cols), bf),
            pltpu.VMEM((chunks, total_rows, cols), bf),
            pltpu.VMEM((total_rows, 2 * block), f32),
            pltpu.VMEM((total_rows, block), f32),
            pltpu.VMEM((block, total_rows), bf),
            pltpu.VMEM((total_rows, 2 * block), bf),
            pltpu.VMEM((chunks, 2, 2, depth, rows, cols), bf),
            pltpu.VMEM((chunks, 2, depth, rows, cols), bf),
            pltpu.VMEM((chunks, depth, rows, cols), bf),
            pltpu.VMEM((chunks, depth, rows, cols), f32),
            pltpu.VMEM((chunks, depth, rows, cols), bf),
            pltpu.VMEM((chunks, depth, rows, cols), bf),
            pltpu.VMEM((chunks, depth - 1, rows, cols), bf),
            dma((chunks,)), dma((chunks,)), dma((chunks,)), dma((chunks,)),
            dma((chunks,)), dma((chunks,)),
            dma((chunks,)), dma((chunks,)),
            dma((chunks,)), dma((chunks,)),
            dma((depth - 1, chunks)), dma((depth - 1, chunks)),
            pltpu.VMEM((helped, 2, 2, depth, share, cols), bf),
            pltpu.VMEM((total_rows, 2 * block), bf),
            dma((1,)), dma((1,)),
            dma((helped,)), dma((helped,)),
            dma((depth - 1, helped)), dma((depth - 1, helped)),
            dma((helped,)), dma((helped,)),
            dma((helped,)), dma((helped,)),
        ],
        compiler_params=pltpu.CompilerParams(
            collective_id=0, has_side_effects=True, vmem_limit_bytes=60 * 1024 * 1024),
        cost_estimate=pl.CostEstimate(
            flops=12 * total_rows * block * width, bytes_accessed=2 * tall * width + 10 * total_rows * width,
            transcendentals=total_rows * block),
    )(acts.reshape(total_rows, width), out_grad.reshape(total_rows, width), params[0])
    in_grad, nm, ns, up = pl.pallas_call(
        finish_kernel,
        out_shape=[jax.ShapeDtypeStruct((total_rows, width), bf)] + [jax.ShapeDtypeStruct(flat, f32)] * 3,
        in_specs=[vmem] * 4,
        out_specs=[hbm] * 4,
        scratch_shapes=[pltpu.VMEM(flat, f32)] * 3 + [dma((4,))],
        compiler_params=pltpu.CompilerParams(vmem_limit_bytes=60 * 1024 * 1024),
        cost_estimate=pl.CostEstimate(flops=0, bytes_accessed=4 * total_rows * width, transcendentals=0),
    )(sent, grad, moment.reshape(flat), second.reshape(flat))
    return (in_grad.reshape(acts.shape), nm.reshape(moment.shape), ns.reshape(moment.shape), up.reshape(moment.shape))


def fits(sizes, acts, params):
    count, block = sizes["dp"], params.shape[1] // 3
    micro_rows = acts.shape[1] * acts.shape[2] // count
    return (sizes["pipe"] == 2 and acts.shape[3] >= 1408 and count % 4 == 0 and count >= 8 and block % (16 * count) == 0 and block % 128 == 0
            and micro_rows % 128 == 0 and acts.shape[2] // count % 16 == 0 and chunk_width(acts.shape[3]) > 0)


def from_behind(value, axis, steps):
    count = lax.axis_size(axis)
    leading, last = (max(0, -steps), min(count, count - steps))
    return lax.ppermute(value, axis, [(source, source + steps) for source in range(leading, last)])


def backward(inputs, grad_rows, weights_in, weights_down):
    block_size = weights_down.shape[0]
    gate_up = lax.dot_general(
        inputs, weights_in, (((1,), (1,)), ((), ())), preferred_element_type=jnp.float32
    )
    gate_values = gate_up[:, :block_size]
    up_values = gate_up[:, block_size:]
    sigmoid_gate = jax.nn.sigmoid(gate_values)
    activated = gate_values * sigmoid_gate
    d_hidden = lax.dot_general(
        grad_rows, weights_down, (((1,), (1,)), ((), ())), preferred_element_type=jnp.float32
    )
    d_gate = d_hidden * up_values * sigmoid_gate * (1.0 + gate_values * (1.0 - sigmoid_gate))
    d_up = d_hidden * activated
    d_gate_up = jnp.concatenate([d_gate, d_up], axis=1).astype(jnp.bfloat16)
    hidden = (activated * up_values).astype(jnp.bfloat16)
    passed = grad_rows.astype(jnp.float32) + jnp.dot(
        d_gate_up, weights_in, preferred_element_type=jnp.float32
    )
    return (passed.astype(jnp.bfloat16), hidden)


def place_slot(stack, value, slot_index, active):
    previous = lax.dynamic_index_in_dim(stack, slot_index, 0, keepdims=False)
    return lax.dynamic_update_index_in_dim(stack, jnp.where(active, value, previous), slot_index, 0)


def weight_terms(hidden, grad_rows):
    lower = lax.dot_general(
        hidden, grad_rows, (((0,), (0,)), ((), ())), preferred_element_type=jnp.float32
    )
    return lower.reshape(-1)


def local(acts, out_grad, params, moment, second):
    sections = lax.axis_size("pipe")
    section_index = lax.axis_index("pipe")
    inputs = acts[0]
    micro_count = inputs.shape[0]
    tok_rows = inputs.shape[1]
    weights = params[0]
    block_size = weights.shape[0] // 3
    weights_in = weights[: 2 * block_size]
    weights_down = weights[2 * block_size :]
    in_grads = jnp.zeros_like(inputs)
    arrived = jnp.zeros_like(inputs)
    hiddens = jnp.zeros((micro_count, tok_rows, block_size), jnp.bfloat16)
    incoming = jnp.zeros_like(inputs[0])
    tick_count = sections + micro_count - 1
    for tick_index in range(tick_count):
        offset = tick_index - (sections - 1) + section_index
        active = jnp.logical_and(offset >= 0, offset < micro_count)
        slot_index = jnp.clip(offset, 0, micro_count - 1)
        current = lax.dynamic_index_in_dim(inputs, slot_index, 0, keepdims=False)
        top_grad = lax.dynamic_index_in_dim(out_grad, slot_index, 0, keepdims=False)
        grad_rows = jnp.where(section_index == sections - 1, top_grad, incoming)

        def working(current=current, grad_rows=grad_rows):
            return backward(current, grad_rows, weights_in, weights_down)

        def resting(current=current):
            return (jnp.zeros_like(current), jnp.zeros((tok_rows, block_size), jnp.bfloat16))

        passed, hidden = lax.cond(active, working, resting)
        in_grads = place_slot(in_grads, passed, slot_index, active)
        arrived = place_slot(arrived, grad_rows, slot_index, active)
        hiddens = place_slot(hiddens, hidden, slot_index, active)
        if tick_index + 1 < tick_count:
            incoming = from_behind(passed, "pipe", -1)
    row_count = micro_count * tok_rows
    term = weight_terms(hiddens.reshape(row_count, block_size), arrived.reshape(row_count, -1))
    summed = lax.psum_scatter(term, "dp", scatter_dimension=0, tiled=True)
    grad_scale = float(row_count * lax.axis_size("dp")) ** (-0.5)
    gradient = summed * grad_scale
    new_moment = 0.9 * moment[0] + 0.1 * gradient
    new_second = 0.999 * second[0] + 0.001 * gradient * gradient
    update = new_moment / (1.0 - 0.9**10) / (jnp.sqrt(new_second / (1.0 - 0.999**10)) + 1e-08)
    return (in_grads[None], new_moment[None], new_second[None], update[None])


def solution(mesh):
    placed = (
        P("pipe", None, "dp", None),
        P(None, "dp", None),
        P("pipe", None, None),
        P("pipe", "dp"),
        P("pipe", "dp"),
    )
    outs = (P("pipe", None, "dp", None), P("pipe", "dp"), P("pipe", "dp"), P("pipe", "dp"))

    def run(acts, out_grad, params, moment, second):
        body = fused if fits(mesh.shape, acts, params) else local
        return jax.shard_map(body, mesh=mesh, in_specs=placed, out_specs=outs, check_vma=False)(
            acts, out_grad, params, moment, second)

    return run
```

```python
import functools

import jax
import jax.numpy as jnp
from jax import lax
from jax.experimental import pallas as pl
from jax.experimental.pallas import tpu as pltpu
from jax.sharding import PartitionSpec as P

MESH = pl.DeviceIdType.MESH
NT = (((1,), (1,)), ((), ()))


def chunk_width(width):
    return max((w for w in (128, 256, 384, 512) if width % w == 0), default=0)


def kernel(dims, x_hbm, g_hbm, w_hbm, out_hbm, grad_ref,
           x, g, w, ig, gu, dh, hid, dgu, part, r1, send2, own, r2, send3, r3,
           load_x, load_g, load_w, store, sy, ry, s1, q1, s2, q2, s3, q3):
    sections, count, cols, chunks, rows, grad_scale = dims
    depth = count // 4
    lag = 2
    block = hid.shape[0]
    sec = lax.axis_index("pipe")
    me = lax.axis_index("dp")
    core, xx, zz = lax.rem(me, 2), lax.rem(me // 2, 2), me // 4
    last = sec == sections - 1
    core_peer = me + 1 - 2 * core
    x_peer = me + 2 - 4 * xx
    z_peers = [me + 4 * (lax.rem(zz + j, depth) - zz) for j in range(1, depth)]

    def at(c):
        return pl.ds(pl.multiple_of(c * cols, cols), cols)

    def loads(c):
        return (pltpu.make_async_copy(w_hbm.at[:, at(c)], w.at[c], load_w.at[c]),
                pltpu.make_async_copy(x_hbm.at[:, at(c)], x.at[c], load_x.at[c]))

    def load_grad(c):
        return pltpu.make_async_copy(g_hbm.at[:, at(c)], g.at[c], load_g.at[c])

    def relay(c):
        return pltpu.make_async_remote_copy(
            ig.at[c], g.at[c], sy.at[c], ry.at[c],
            device_id={"pipe": lax.max(sec - 1, 0), "dp": me}, device_id_type=MESH)

    def stage1(c):
        return pltpu.make_async_remote_copy(
            part.at[c, 1 - core], r1.at[c], s1.at[c], q1.at[c],
            device_id={"pipe": sec, "dp": core_peer}, device_id_type=MESH)

    def stage2(c):
        return pltpu.make_async_remote_copy(
            send2.at[c], r2.at[c], s2.at[c], q2.at[c],
            device_id={"pipe": sec, "dp": x_peer}, device_id_type=MESH)

    def stage3(c, j):
        return pltpu.make_async_remote_copy(
            send3.at[c, lax.rem(zz + j + 1, depth)], r3.at[c, j], s3.at[j, c], q3.at[j, c],
            device_id={"pipe": sec, "dp": z_peers[j]}, device_id_type=MESH)

    def result(c):
        return pltpu.make_async_copy(ig.at[c], out_hbm.at[:, at(c)], store.at[c])

    def each(body, low=0, high=chunks):
        def step(c, carry):
            body(c)
            return carry
        lax.fori_loop(low, high, step, 0)

    barrier = pltpu.get_barrier_semaphore()
    for peer in [core_peer, x_peer] + z_peers:
        pl.semaphore_signal(barrier, inc=1, device_id={"pipe": sec, "dp": peer}, device_id_type=MESH)

    @pl.when(sec > 0)
    def _():
        pl.semaphore_signal(barrier, inc=1, device_id={"pipe": lax.max(sec - 1, 0), "dp": me}, device_id_type=MESH)

    @pl.when(jnp.logical_not(last))
    def _():
        pl.semaphore_signal(barrier, inc=1, device_id={"pipe": lax.min(sec + 1, sections - 1), "dp": me}, device_id_type=MESH)

    def begin(c):
        for copy in loads(c):
            copy.start()

        @pl.when(last)
        def _():
            load_grad(c).start()

    each(begin)
    gu[...] = jnp.zeros_like(gu)
    dh[...] = jnp.zeros_like(dh)

    def add_hidden_grad(c):
        dh[...] += lax.dot_general(g[c], w[c, 2 * block:, :], NT, preferred_element_type=jnp.float32)

    def forward(c):
        for copy in loads(c):
            copy.wait()
        gu[...] += lax.dot_general(x[c], w[c, : 2 * block, :], NT, preferred_element_type=jnp.float32)

        @pl.when(last)
        def _():
            load_grad(c).wait()
            add_hidden_grad(c)

    each(forward)
    gate, up = gu[:, :block], gu[:, block:]
    hid[...] = (gate * jax.nn.sigmoid(gate) * up).T.astype(jnp.bfloat16)

    pl.semaphore_wait(barrier, 1 + depth + lax.min(sec, 1) + lax.min(sections - 1 - sec, 1))

    def input_grad():
        gate_v, up_v, d = gu[:, :block], gu[:, block:], dh[...]
        sg = jax.nn.sigmoid(gate_v)
        dgu[:, :block] = (d * up_v * sg * (1.0 + gate_v * (1.0 - sg))).astype(jnp.bfloat16)
        dgu[:, block:] = (d * gate_v * sg).astype(jnp.bfloat16)

        def one(c):
            ig[c] = (g[c].astype(jnp.float32) + jnp.dot(
                dgu[...], w[c, : 2 * block, :], preferred_element_type=jnp.float32)).astype(jnp.bfloat16)

            @pl.when(sec > 0)
            def _():
                relay(c).start()

            result(c).start()

        each(one)

    @pl.when(last)
    def _():
        input_grad()

    def step(t):
        @pl.when(t < chunks)
        def _():
            @pl.when(jnp.logical_not(last))
            def _():
                relay(t).wait_recv()

            term = jnp.dot(hid[...], g[t], preferred_element_type=jnp.float32)
            for owner in range(count):
                part[t, owner % 2, owner // 2 % 2, owner // 4] = term[
                    owner * rows:(owner + 1) * rows].astype(jnp.bfloat16)
            stage1(t).start()

            @pl.when(jnp.logical_not(last))
            def _():
                add_hidden_grad(t)

        @pl.when(jnp.logical_and(t >= lag, t < chunks + lag))
        def _():
            c = t - lag
            stage1(c).wait_recv()
            for z in range(depth):
                send2[c, z] = (part[c, core, 1 - xx, z].astype(jnp.float32)
                                      + r1[c, 1 - xx, z].astype(jnp.float32)).astype(jnp.bfloat16)
            stage2(c).start()
            for z in range(depth):
                own[c, z] = (part[c, core, xx, z].astype(jnp.float32)
                                    + r1[c, xx, z].astype(jnp.float32))

        @pl.when(jnp.logical_and(t >= 2 * lag, t < chunks + 2 * lag))
        def _():
            c = t - 2 * lag
            stage2(c).wait_recv()
            for z in range(depth):
                total = own[c, z] + r2[c, z].astype(jnp.float32)
                own[c, z] = total
                send3[c, z] = total.astype(jnp.bfloat16)
            for j in range(depth - 1):
                stage3(c, j).start()

        @pl.when(jnp.logical_and(t == chunks + lag - 1, jnp.logical_not(last)))
        def _():
            input_grad()

        @pl.when(t >= 3 * lag)
        def _():
            c = t - 3 * lag
            total = own[c, zz]
            for j in range(depth - 1):
                stage3(c, j).wait_recv()
            for j in range(depth - 1):
                total = total + r3[c, j].astype(jnp.float32)
            grad = total * grad_scale
            lanes = cols // 128
            for k in range(lanes):
                where = pl.ds(c * lanes + k, rows, stride=chunks * lanes)
                grad_ref[where, :] = grad[:, k * 128:(k + 1) * 128]

    each(step, 0, chunks + 3 * lag)

    def finish(c):
        stage1(c).wait_send()
        stage2(c).wait_send()
        for j in range(depth - 1):
            stage3(c, j).wait_send()

        @pl.when(sec > 0)
        def _():
            relay(c).wait_send()

        result(c).wait()

    each(finish)


def finish_kernel(sent_ref, grad_ref, m_ref, s_ref, out_hbm, nm_hbm, ns_hbm, up_hbm, nm, ns, up, sem):
    pairs = ((sent_ref, out_hbm), (nm, nm_hbm), (ns, ns_hbm), (up, up_hbm))
    copies = [pltpu.make_async_copy(source, target, sem.at[i]) for i, (source, target) in enumerate(pairs)]
    copies[0].start()
    grad = grad_ref[...]
    nm[...] = 0.9 * m_ref[...] + 0.1 * grad
    copies[1].start()
    ns[...] = 0.999 * s_ref[...] + 0.001 * grad * grad
    copies[2].start()
    up[...] = nm[...] / (1.0 - 0.9**10) / (jnp.sqrt(ns[...] / (1.0 - 0.999**10)) + 1e-08)
    copies[3].start()
    for copy in copies:
        copy.wait()


def fused(acts, out_grad, params, moment, second):
    sections, count = lax.axis_size("pipe"), lax.axis_size("dp")
    _, micro, tok, width = acts.shape
    tall = params.shape[1]
    block = tall // 3
    total_rows = micro * tok
    cols = chunk_width(width)
    chunks = width // cols
    rows = block // count
    depth = count // 4
    flat = (rows * width // 128, 128)
    grad_scale = float(total_rows * count) ** (-0.5)
    bf, f32 = jnp.bfloat16, jnp.float32
    dma = pltpu.SemaphoreType.DMA
    anywhere = pl.BlockSpec(memory_space=pl.ANY)
    vmem = pl.BlockSpec(memory_space=pltpu.VMEM)
    hbm = pl.BlockSpec(memory_space=pltpu.HBM)
    sent, grad = pl.pallas_call(
        functools.partial(kernel, (sections, count, cols, chunks, rows, grad_scale)),
        out_shape=[jax.ShapeDtypeStruct((total_rows, width), bf)] + [jax.ShapeDtypeStruct(flat, f32)],
        in_specs=[hbm] * 3,
        out_specs=[anywhere, vmem],
        scratch_shapes=[
            pltpu.VMEM((chunks, total_rows, cols), bf),
            pltpu.VMEM((chunks, total_rows, cols), bf),
            pltpu.VMEM((chunks, tall, cols), bf),
            pltpu.VMEM((chunks, total_rows, cols), bf),
            pltpu.VMEM((total_rows, 2 * block), f32),
            pltpu.VMEM((total_rows, block), f32),
            pltpu.VMEM((block, total_rows), bf),
            pltpu.VMEM((total_rows, 2 * block), bf),
            pltpu.VMEM((chunks, 2, 2, depth, rows, cols), bf),
            pltpu.VMEM((chunks, 2, depth, rows, cols), bf),
            pltpu.VMEM((chunks, depth, rows, cols), bf),
            pltpu.VMEM((chunks, depth, rows, cols), f32),
            pltpu.VMEM((chunks, depth, rows, cols), bf),
            pltpu.VMEM((chunks, depth, rows, cols), bf),
            pltpu.VMEM((chunks, depth - 1, rows, cols), bf),
            dma((chunks,)), dma((chunks,)), dma((chunks,)), dma((chunks,)),
            dma((chunks,)), dma((chunks,)),
            dma((chunks,)), dma((chunks,)),
            dma((chunks,)), dma((chunks,)),
            dma((depth - 1, chunks)), dma((depth - 1, chunks)),
        ],
        compiler_params=pltpu.CompilerParams(
            collective_id=0, has_side_effects=True, vmem_limit_bytes=60 * 1024 * 1024),
        cost_estimate=pl.CostEstimate(
            flops=12 * total_rows * block * width, bytes_accessed=2 * tall * width + 10 * total_rows * width,
            transcendentals=total_rows * block),
    )(acts.reshape(total_rows, width), out_grad.reshape(total_rows, width), params[0])
    in_grad, nm, ns, up = pl.pallas_call(
        finish_kernel,
        out_shape=[jax.ShapeDtypeStruct((total_rows, width), bf)] + [jax.ShapeDtypeStruct(flat, f32)] * 3,
        in_specs=[vmem] * 4,
        out_specs=[hbm] * 4,
        scratch_shapes=[pltpu.VMEM(flat, f32)] * 3 + [dma((4,))],
        compiler_params=pltpu.CompilerParams(vmem_limit_bytes=60 * 1024 * 1024),
        cost_estimate=pl.CostEstimate(flops=0, bytes_accessed=4 * total_rows * width, transcendentals=0),
    )(sent, grad, moment.reshape(flat), second.reshape(flat))
    return (in_grad.reshape(acts.shape), nm.reshape(moment.shape), ns.reshape(moment.shape), up.reshape(moment.shape))


def fits(sizes, acts, params):
    count, block = sizes["dp"], params.shape[1] // 3
    micro_rows = acts.shape[1] * acts.shape[2] // count
    return (count % 4 == 0 and count >= 8 and block % (16 * count) == 0 and block % 128 == 0
            and micro_rows % 128 == 0 and acts.shape[2] // count % 16 == 0 and chunk_width(acts.shape[3]) > 0)


def from_behind(value, axis, steps):
    count = lax.axis_size(axis)
    leading, last = (max(0, -steps), min(count, count - steps))
    return lax.ppermute(value, axis, [(source, source + steps) for source in range(leading, last)])


def backward(inputs, grad_rows, weights_in, weights_down):
    block_size = weights_down.shape[0]
    gate_up = lax.dot_general(
        inputs, weights_in, (((1,), (1,)), ((), ())), preferred_element_type=jnp.float32
    )
    gate_values = gate_up[:, :block_size]
    up_values = gate_up[:, block_size:]
    sigmoid_gate = jax.nn.sigmoid(gate_values)
    activated = gate_values * sigmoid_gate
    d_hidden = lax.dot_general(
        grad_rows, weights_down, (((1,), (1,)), ((), ())), preferred_element_type=jnp.float32
    )
    d_gate = d_hidden * up_values * sigmoid_gate * (1.0 + gate_values * (1.0 - sigmoid_gate))
    d_up = d_hidden * activated
    d_gate_up = jnp.concatenate([d_gate, d_up], axis=1).astype(jnp.bfloat16)
    hidden = (activated * up_values).astype(jnp.bfloat16)
    passed = grad_rows.astype(jnp.float32) + jnp.dot(
        d_gate_up, weights_in, preferred_element_type=jnp.float32
    )
    return (passed.astype(jnp.bfloat16), hidden)


def place_slot(stack, value, slot_index, active):
    previous = lax.dynamic_index_in_dim(stack, slot_index, 0, keepdims=False)
    return lax.dynamic_update_index_in_dim(stack, jnp.where(active, value, previous), slot_index, 0)


def weight_terms(hidden, grad_rows):
    lower = lax.dot_general(
        hidden, grad_rows, (((0,), (0,)), ((), ())), preferred_element_type=jnp.float32
    )
    return lower.reshape(-1)


def local(acts, out_grad, params, moment, second):
    sections = lax.axis_size("pipe")
    section_index = lax.axis_index("pipe")
    inputs = acts[0]
    micro_count = inputs.shape[0]
    tok_rows = inputs.shape[1]
    weights = params[0]
    block_size = weights.shape[0] // 3
    weights_in = weights[: 2 * block_size]
    weights_down = weights[2 * block_size :]
    in_grads = jnp.zeros_like(inputs)
    arrived = jnp.zeros_like(inputs)
    hiddens = jnp.zeros((micro_count, tok_rows, block_size), jnp.bfloat16)
    incoming = jnp.zeros_like(inputs[0])
    tick_count = sections + micro_count - 1
    for tick_index in range(tick_count):
        offset = tick_index - (sections - 1) + section_index
        active = jnp.logical_and(offset >= 0, offset < micro_count)
        slot_index = jnp.clip(offset, 0, micro_count - 1)
        current = lax.dynamic_index_in_dim(inputs, slot_index, 0, keepdims=False)
        top_grad = lax.dynamic_index_in_dim(out_grad, slot_index, 0, keepdims=False)
        grad_rows = jnp.where(section_index == sections - 1, top_grad, incoming)

        def working(current=current, grad_rows=grad_rows):
            return backward(current, grad_rows, weights_in, weights_down)

        def resting(current=current):
            return (jnp.zeros_like(current), jnp.zeros((tok_rows, block_size), jnp.bfloat16))

        passed, hidden = lax.cond(active, working, resting)
        in_grads = place_slot(in_grads, passed, slot_index, active)
        arrived = place_slot(arrived, grad_rows, slot_index, active)
        hiddens = place_slot(hiddens, hidden, slot_index, active)
        if tick_index + 1 < tick_count:
            incoming = from_behind(passed, "pipe", -1)
    row_count = micro_count * tok_rows
    term = weight_terms(hiddens.reshape(row_count, block_size), arrived.reshape(row_count, -1))
    summed = lax.psum_scatter(term, "dp", scatter_dimension=0, tiled=True)
    grad_scale = float(row_count * lax.axis_size("dp")) ** (-0.5)
    gradient = summed * grad_scale
    new_moment = 0.9 * moment[0] + 0.1 * gradient
    new_second = 0.999 * second[0] + 0.001 * gradient * gradient
    update = new_moment / (1.0 - 0.9**10) / (jnp.sqrt(new_second / (1.0 - 0.999**10)) + 1e-08)
    return (in_grads[None], new_moment[None], new_second[None], update[None])


def solution(mesh):
    placed = (
        P("pipe", None, "dp", None),
        P(None, "dp", None),
        P("pipe", None, None),
        P("pipe", "dp"),
        P("pipe", "dp"),
    )
    outs = (P("pipe", None, "dp", None), P("pipe", "dp"), P("pipe", "dp"), P("pipe", "dp"))

    def run(acts, out_grad, params, moment, second):
        body = fused if fits(mesh.shape, acts, params) else local
        return jax.shard_map(body, mesh=mesh, in_specs=placed, out_specs=outs, check_vma=False)(
            acts, out_grad, params, moment, second)

    return run
```

```python
import functools

import jax
import jax.numpy as jnp
from jax import lax
from jax.experimental import pallas as pl
from jax.experimental.pallas import tpu as pltpu
from jax.sharding import PartitionSpec as P

MESH = pl.DeviceIdType.MESH
NT = (((1,), (1,)), ((), ()))


def chunk_width(width):
    return max((w for w in (128, 256, 384, 512) if width % w == 0), default=0)


def kernel(dims, x_hbm, g_hbm, w_hbm, out_hbm, grad_ref,
           x, g, w, ig, gu, dh, hid, dgu, part, r1, send2, own, r2, send3, r3,
           load_x, load_g, load_w, store, sy, ry, s1, q1, s2, q2, s3, q3):
    sections, count, cols, chunks, rows, grad_scale = dims
    depth = count // 4
    lag = 2
    block = hid.shape[0]
    sec = lax.axis_index("pipe")
    me = lax.axis_index("dp")
    core, xx, zz = lax.rem(me, 2), lax.rem(me // 2, 2), me // 4
    last = sec == sections - 1
    core_peer = me + 1 - 2 * core
    x_peer = me + 2 - 4 * xx
    z_peers = [me + 4 * (lax.rem(zz + j, depth) - zz) for j in range(1, depth)]

    def at(c):
        return pl.ds(pl.multiple_of(c * cols, cols), cols)

    def loads(c):
        return (pltpu.make_async_copy(w_hbm.at[:, at(c)], w.at[c], load_w.at[c]),
                pltpu.make_async_copy(x_hbm.at[:, at(c)], x.at[c], load_x.at[c]))

    def load_grad(c):
        return pltpu.make_async_copy(g_hbm.at[:, at(c)], g.at[c], load_g.at[c])

    def relay(c):
        return pltpu.make_async_remote_copy(
            ig.at[c], g.at[c], sy.at[c], ry.at[c],
            device_id={"pipe": lax.max(sec - 1, 0), "dp": me}, device_id_type=MESH)

    def stage1(c):
        return pltpu.make_async_remote_copy(
            part.at[c, 1 - core], r1.at[c], s1.at[c], q1.at[c],
            device_id={"pipe": sec, "dp": core_peer}, device_id_type=MESH)

    def stage2(c):
        return pltpu.make_async_remote_copy(
            send2.at[c], r2.at[c], s2.at[c], q2.at[c],
            device_id={"pipe": sec, "dp": x_peer}, device_id_type=MESH)

    def stage3(c, j):
        return pltpu.make_async_remote_copy(
            send3.at[c, lax.rem(zz + j + 1, depth)], r3.at[c, j], s3.at[j, c], q3.at[j, c],
            device_id={"pipe": sec, "dp": z_peers[j]}, device_id_type=MESH)

    def result(c):
        return pltpu.make_async_copy(ig.at[c], out_hbm.at[:, at(c)], store.at[c])

    def each(body, low=0, high=chunks):
        def step(c, carry):
            body(c)
            return carry
        lax.fori_loop(low, high, step, 0)

    barrier = pltpu.get_barrier_semaphore()
    for peer in [core_peer, x_peer] + z_peers:
        pl.semaphore_signal(barrier, inc=1, device_id={"pipe": sec, "dp": peer}, device_id_type=MESH)

    @pl.when(sec > 0)
    def _():
        pl.semaphore_signal(barrier, inc=1, device_id={"pipe": lax.max(sec - 1, 0), "dp": me}, device_id_type=MESH)

    @pl.when(jnp.logical_not(last))
    def _():
        pl.semaphore_signal(barrier, inc=1, device_id={"pipe": lax.min(sec + 1, sections - 1), "dp": me}, device_id_type=MESH)

    def begin(c):
        for copy in loads(c):
            copy.start()

        @pl.when(last)
        def _():
            load_grad(c).start()

    each(begin)
    gu[...] = jnp.zeros_like(gu)
    dh[...] = jnp.zeros_like(dh)

    def add_hidden_grad(c):
        dh[...] += lax.dot_general(g[c], w[c, 2 * block:, :], NT, preferred_element_type=jnp.float32)

    def forward(c):
        for copy in loads(c):
            copy.wait()
        gu[...] += lax.dot_general(x[c], w[c, : 2 * block, :], NT, preferred_element_type=jnp.float32)

        @pl.when(last)
        def _():
            load_grad(c).wait()
            add_hidden_grad(c)

    each(forward)
    gate, up = gu[:, :block], gu[:, block:]
    hid[...] = (gate * jax.nn.sigmoid(gate) * up).T.astype(jnp.bfloat16)

    pl.semaphore_wait(barrier, 1 + depth + lax.min(sec, 1) + lax.min(sections - 1 - sec, 1))

    def input_grad():
        gate_v, up_v, d = gu[:, :block], gu[:, block:], dh[...]
        sg = jax.nn.sigmoid(gate_v)
        dgu[:, :block] = (d * up_v * sg * (1.0 + gate_v * (1.0 - sg))).astype(jnp.bfloat16)
        dgu[:, block:] = (d * gate_v * sg).astype(jnp.bfloat16)

        def one(c):
            ig[c] = (g[c].astype(jnp.float32) + jnp.dot(
                dgu[...], w[c, : 2 * block, :], preferred_element_type=jnp.float32)).astype(jnp.bfloat16)

            @pl.when(sec > 0)
            def _():
                relay(c).start()

            result(c).start()

        each(one)

    @pl.when(last)
    def _():
        input_grad()

    def step(t):
        @pl.when(t < chunks)
        def _():
            @pl.when(jnp.logical_not(last))
            def _():
                relay(t).wait_recv()

            term = jnp.dot(hid[...], g[t], preferred_element_type=jnp.float32)
            for owner in range(count):
                part[t, owner % 2, owner // 2 % 2, owner // 4] = term[
                    owner * rows:(owner + 1) * rows].astype(jnp.bfloat16)
            stage1(t).start()

            @pl.when(jnp.logical_not(last))
            def _():
                add_hidden_grad(t)

        @pl.when(jnp.logical_and(t >= lag, t < chunks + lag))
        def _():
            c = t - lag
            stage1(c).wait_recv()
            for z in range(depth):
                send2[c, z] = (part[c, core, 1 - xx, z].astype(jnp.float32)
                                      + r1[c, 1 - xx, z].astype(jnp.float32)).astype(jnp.bfloat16)
            stage2(c).start()
            for z in range(depth):
                own[c, z] = (part[c, core, xx, z].astype(jnp.float32)
                                    + r1[c, xx, z].astype(jnp.float32))

        @pl.when(jnp.logical_and(t >= 2 * lag, t < chunks + 2 * lag))
        def _():
            c = t - 2 * lag
            stage2(c).wait_recv()
            for z in range(depth):
                total = own[c, z] + r2[c, z].astype(jnp.float32)
                own[c, z] = total
                send3[c, z] = total.astype(jnp.bfloat16)
            for j in range(depth - 1):
                stage3(c, j).start()

        @pl.when(jnp.logical_and(t == chunks + 2 * lag - 1, jnp.logical_not(last)))
        def _():
            input_grad()

        @pl.when(t >= 3 * lag)
        def _():
            c = t - 3 * lag
            total = own[c, zz]
            for j in range(depth - 1):
                stage3(c, j).wait_recv()
            for j in range(depth - 1):
                total = total + r3[c, j].astype(jnp.float32)
            grad = total * grad_scale
            lanes = cols // 128
            for k in range(lanes):
                where = pl.ds(c * lanes + k, rows, stride=chunks * lanes)
                grad_ref[where, :] = grad[:, k * 128:(k + 1) * 128]

    each(step, 0, chunks + 3 * lag)

    def finish(c):
        stage1(c).wait_send()
        stage2(c).wait_send()
        for j in range(depth - 1):
            stage3(c, j).wait_send()

        @pl.when(sec > 0)
        def _():
            relay(c).wait_send()

        result(c).wait()

    each(finish)


def finish_kernel(sent_ref, grad_ref, m_ref, s_ref, out_hbm, nm_hbm, ns_hbm, up_hbm, nm, ns, up, sem):
    pairs = ((sent_ref, out_hbm), (nm, nm_hbm), (ns, ns_hbm), (up, up_hbm))
    copies = [pltpu.make_async_copy(source, target, sem.at[i]) for i, (source, target) in enumerate(pairs)]
    copies[0].start()
    grad = grad_ref[...]
    nm[...] = 0.9 * m_ref[...] + 0.1 * grad
    copies[1].start()
    ns[...] = 0.999 * s_ref[...] + 0.001 * grad * grad
    copies[2].start()
    up[...] = nm[...] / (1.0 - 0.9**10) / (jnp.sqrt(ns[...] / (1.0 - 0.999**10)) + 1e-08)
    copies[3].start()
    for copy in copies:
        copy.wait()


def fused(acts, out_grad, params, moment, second):
    sections, count = lax.axis_size("pipe"), lax.axis_size("dp")
    _, micro, tok, width = acts.shape
    tall = params.shape[1]
    block = tall // 3
    total_rows = micro * tok
    cols = chunk_width(width)
    chunks = width // cols
    rows = block // count
    depth = count // 4
    flat = (rows * width // 128, 128)
    grad_scale = float(total_rows * count) ** (-0.5)
    bf, f32 = jnp.bfloat16, jnp.float32
    dma = pltpu.SemaphoreType.DMA
    anywhere = pl.BlockSpec(memory_space=pl.ANY)
    vmem = pl.BlockSpec(memory_space=pltpu.VMEM)
    hbm = pl.BlockSpec(memory_space=pltpu.HBM)
    sent, grad = pl.pallas_call(
        functools.partial(kernel, (sections, count, cols, chunks, rows, grad_scale)),
        out_shape=[jax.ShapeDtypeStruct((total_rows, width), bf)] + [jax.ShapeDtypeStruct(flat, f32)],
        in_specs=[hbm] * 3,
        out_specs=[anywhere, vmem],
        scratch_shapes=[
            pltpu.VMEM((chunks, total_rows, cols), bf),
            pltpu.VMEM((chunks, total_rows, cols), bf),
            pltpu.VMEM((chunks, tall, cols), bf),
            pltpu.VMEM((chunks, total_rows, cols), bf),
            pltpu.VMEM((total_rows, 2 * block), f32),
            pltpu.VMEM((total_rows, block), f32),
            pltpu.VMEM((block, total_rows), bf),
            pltpu.VMEM((total_rows, 2 * block), bf),
            pltpu.VMEM((chunks, 2, 2, depth, rows, cols), bf),
            pltpu.VMEM((chunks, 2, depth, rows, cols), bf),
            pltpu.VMEM((chunks, depth, rows, cols), bf),
            pltpu.VMEM((chunks, depth, rows, cols), f32),
            pltpu.VMEM((chunks, depth, rows, cols), bf),
            pltpu.VMEM((chunks, depth, rows, cols), bf),
            pltpu.VMEM((chunks, depth - 1, rows, cols), bf),
            dma((chunks,)), dma((chunks,)), dma((chunks,)), dma((chunks,)),
            dma((chunks,)), dma((chunks,)),
            dma((chunks,)), dma((chunks,)),
            dma((chunks,)), dma((chunks,)),
            dma((depth - 1, chunks)), dma((depth - 1, chunks)),
        ],
        compiler_params=pltpu.CompilerParams(
            collective_id=0, has_side_effects=True, vmem_limit_bytes=60 * 1024 * 1024),
        cost_estimate=pl.CostEstimate(
            flops=12 * total_rows * block * width, bytes_accessed=2 * tall * width + 10 * total_rows * width,
            transcendentals=total_rows * block),
    )(acts.reshape(total_rows, width), out_grad.reshape(total_rows, width), params[0])
    in_grad, nm, ns, up = pl.pallas_call(
        finish_kernel,
        out_shape=[jax.ShapeDtypeStruct((total_rows, width), bf)] + [jax.ShapeDtypeStruct(flat, f32)] * 3,
        in_specs=[vmem] * 4,
        out_specs=[hbm] * 4,
        scratch_shapes=[pltpu.VMEM(flat, f32)] * 3 + [dma((4,))],
        compiler_params=pltpu.CompilerParams(vmem_limit_bytes=60 * 1024 * 1024),
        cost_estimate=pl.CostEstimate(flops=0, bytes_accessed=4 * total_rows * width, transcendentals=0),
    )(sent, grad, moment.reshape(flat), second.reshape(flat))
    return (in_grad.reshape(acts.shape), nm.reshape(moment.shape), ns.reshape(moment.shape), up.reshape(moment.shape))


def fits(sizes, acts, params):
    count, block = sizes["dp"], params.shape[1] // 3
    micro_rows = acts.shape[1] * acts.shape[2] // count
    return (count % 4 == 0 and count >= 8 and block % (16 * count) == 0 and block % 128 == 0
            and micro_rows % 128 == 0 and acts.shape[2] // count % 16 == 0 and chunk_width(acts.shape[3]) > 0)


def from_behind(value, axis, steps):
    count = lax.axis_size(axis)
    leading, last = (max(0, -steps), min(count, count - steps))
    return lax.ppermute(value, axis, [(source, source + steps) for source in range(leading, last)])


def backward(inputs, grad_rows, weights_in, weights_down):
    block_size = weights_down.shape[0]
    gate_up = lax.dot_general(
        inputs, weights_in, (((1,), (1,)), ((), ())), preferred_element_type=jnp.float32
    )
    gate_values = gate_up[:, :block_size]
    up_values = gate_up[:, block_size:]
    sigmoid_gate = jax.nn.sigmoid(gate_values)
    activated = gate_values * sigmoid_gate
    d_hidden = lax.dot_general(
        grad_rows, weights_down, (((1,), (1,)), ((), ())), preferred_element_type=jnp.float32
    )
    d_gate = d_hidden * up_values * sigmoid_gate * (1.0 + gate_values * (1.0 - sigmoid_gate))
    d_up = d_hidden * activated
    d_gate_up = jnp.concatenate([d_gate, d_up], axis=1).astype(jnp.bfloat16)
    hidden = (activated * up_values).astype(jnp.bfloat16)
    passed = grad_rows.astype(jnp.float32) + jnp.dot(
        d_gate_up, weights_in, preferred_element_type=jnp.float32
    )
    return (passed.astype(jnp.bfloat16), hidden)


def place_slot(stack, value, slot_index, active):
    previous = lax.dynamic_index_in_dim(stack, slot_index, 0, keepdims=False)
    return lax.dynamic_update_index_in_dim(stack, jnp.where(active, value, previous), slot_index, 0)


def weight_terms(hidden, grad_rows):
    lower = lax.dot_general(
        hidden, grad_rows, (((0,), (0,)), ((), ())), preferred_element_type=jnp.float32
    )
    return lower.reshape(-1)


def local(acts, out_grad, params, moment, second):
    sections = lax.axis_size("pipe")
    section_index = lax.axis_index("pipe")
    inputs = acts[0]
    micro_count = inputs.shape[0]
    tok_rows = inputs.shape[1]
    weights = params[0]
    block_size = weights.shape[0] // 3
    weights_in = weights[: 2 * block_size]
    weights_down = weights[2 * block_size :]
    in_grads = jnp.zeros_like(inputs)
    arrived = jnp.zeros_like(inputs)
    hiddens = jnp.zeros((micro_count, tok_rows, block_size), jnp.bfloat16)
    incoming = jnp.zeros_like(inputs[0])
    tick_count = sections + micro_count - 1
    for tick_index in range(tick_count):
        offset = tick_index - (sections - 1) + section_index
        active = jnp.logical_and(offset >= 0, offset < micro_count)
        slot_index = jnp.clip(offset, 0, micro_count - 1)
        current = lax.dynamic_index_in_dim(inputs, slot_index, 0, keepdims=False)
        top_grad = lax.dynamic_index_in_dim(out_grad, slot_index, 0, keepdims=False)
        grad_rows = jnp.where(section_index == sections - 1, top_grad, incoming)

        def working(current=current, grad_rows=grad_rows):
            return backward(current, grad_rows, weights_in, weights_down)

        def resting(current=current):
            return (jnp.zeros_like(current), jnp.zeros((tok_rows, block_size), jnp.bfloat16))

        passed, hidden = lax.cond(active, working, resting)
        in_grads = place_slot(in_grads, passed, slot_index, active)
        arrived = place_slot(arrived, grad_rows, slot_index, active)
        hiddens = place_slot(hiddens, hidden, slot_index, active)
        if tick_index + 1 < tick_count:
            incoming = from_behind(passed, "pipe", -1)
    row_count = micro_count * tok_rows
    term = weight_terms(hiddens.reshape(row_count, block_size), arrived.reshape(row_count, -1))
    summed = lax.psum_scatter(term, "dp", scatter_dimension=0, tiled=True)
    grad_scale = float(row_count * lax.axis_size("dp")) ** (-0.5)
    gradient = summed * grad_scale
    new_moment = 0.9 * moment[0] + 0.1 * gradient
    new_second = 0.999 * second[0] + 0.001 * gradient * gradient
    update = new_moment / (1.0 - 0.9**10) / (jnp.sqrt(new_second / (1.0 - 0.999**10)) + 1e-08)
    return (in_grads[None], new_moment[None], new_second[None], update[None])


def solution(mesh):
    placed = (
        P("pipe", None, "dp", None),
        P(None, "dp", None),
        P("pipe", None, None),
        P("pipe", "dp"),
        P("pipe", "dp"),
    )
    outs = (P("pipe", None, "dp", None), P("pipe", "dp"), P("pipe", "dp"), P("pipe", "dp"))

    def run(acts, out_grad, params, moment, second):
        body = fused if fits(mesh.shape, acts, params) else local
        return jax.shard_map(body, mesh=mesh, in_specs=placed, out_specs=outs, check_vma=False)(
            acts, out_grad, params, moment, second)

    return run
```
